32 devices in a mesh: pp: 4 (over x, core), cp: 4 (over z), tp: 2 (over y).
Axes of the slice: x: 2, y: 2, z: 4, core: 2. Of those that a mesh axis runs over, the one named last changes fastest.
Arguments:
- query: bfloat16 [4, 512, 4096], P('pp', 'cp', 'tp'), may hold values from -200 to 200
- key: bfloat16 [4, 512, 256], P('pp', 'cp', 'tp'), may hold values from -6 to 6
- value: bfloat16 [4, 512, 256], P('pp', 'cp', 'tp'), may hold values from -6 to 6
- out_grad: bfloat16 [4, 512, 4096], P('pp', 'cp', 'tp'), may hold values from -24 to 24
- lengths: int32 [6], replicated, may hold values from 1 to 256, 512 in all
- plan: int32 [4, 4], replicated, may hold values from 0 to 3, each once within a row
Outputs:
- handed_grad: bfloat16 [4, 512, 4096], P('pp', 'cp', 'tp')
- key_grad: bfloat16 [4, 512, 256], P('pp', 'cp', 'tp')
- value_grad: bfloat16 [4, 512, 256], P('pp', 'cp', 'tp')
The draws below stay inside these ranges and needn't reach their ends.
Inputs may be any that keep to these rules, and one draw needn't show every extreme that they name: Row s of plan is a permutation: for each of the blocks of 32 tokens of context shard s it names the shard that takes the block.
All inputs are finite; a program needn't handle non-finite values.
Results may differ from the reference program's by a relative error of at most 0.0085.
Values may be sent and summed in bfloat16 or wider, within the bound.
A program may use at most 64 MiB of HBM per device.

```python
import math
import jax
import jax.numpy as jnp
import numpy as np
from jax import lax

HD = 128
NDOC = 6
HEADS = 32
KVH = 2
SEQ = 512
N_PP = 4
N_CP = 4


def shared_draw(key):
    base = jax.random.fold_in(key, 7)
    key_query, key_key = jax.random.split(base)
    queries = jnp.clip(jax.random.normal(key_query, (N_PP, SEQ, HEADS, HD), jnp.float32), -6.0, 6.0)
    keys = jnp.clip(jax.random.normal(key_key, (N_PP, SEQ, KVH, HD), jnp.float32), -6.0, 6.0)
    return (queries.reshape(N_PP, SEQ, HEADS * HD), keys.reshape(N_PP, SEQ, KVH * HD))


def draw_query(key, part):
    return shared_draw(key)[0].astype(jnp.bfloat16)


def draw_key(key, part):
    return shared_draw(key)[1].astype(jnp.bfloat16)


def block_levels(key, dims, cuts, least, high):
    def one(dim, parts):
        steps = jax.random.uniform(jax.random.fold_in(jax.random.fold_in(key, 6), dim), (parts,), jnp.float32, least / len(cuts), high / len(cuts))
        return jnp.repeat(jnp.exp(steps), dims[dim] // parts).reshape((-1,) + (1,) * (len(dims) - dim - 1))

    factor_of = one(*cuts[0])
    for cut in cuts[1:]:
        factor_of = factor_of * one(*cut)
    return factor_of


def length_profile(number_of, total, reach, lean):
    loads = [(1 << 20) // math.isqrt(rank ** lean) + 1 for rank in range(2, number_of + 1)]
    rest, given = total - reach - (number_of - 1), [1] * (number_of - 1)
    while rest > 0:
        movable = [i for i in range(number_of - 1) if given[i] < reach]
        mass, budget = sum([loads[i] for i in movable]), rest
        for i in movable:
            addition = min(reach - given[i], max(1, budget * loads[i] // mass), rest)
            given[i] = given[i] + addition
            rest = rest - addition
    return np.array([reach] + given)


def uneven(rng, number_of, total, bound, slope):
    if number_of == 2:
        one = jax.random.randint(rng, (), max(1, total - bound), min(bound, total - 1) + 1)
        return jnp.stack([one, total - one])
    sizes = jnp.asarray(length_profile(number_of, total, bound, slope), jnp.int32)
    pairs = (number_of - 1) // 2
    giver, receiver = sizes[1:1 + 2 * pairs:2], sizes[2:2 + 2 * pairs:2]
    slack = jnp.minimum(giver - 1, bound - receiver)
    passed = jax.random.randint(jax.random.fold_in(rng, 1), (pairs,), 0, 1 << 20) % (slack + 1)
    sizes = sizes.at[1:1 + 2 * pairs:2].set(giver - passed).at[2:2 + 2 * pairs:2].set(receiver + passed)
    return sizes[jax.random.permutation(jax.random.fold_in(rng, 2), number_of)]


def noise(own_key, extent, spread, reach, cuts=(), held_as=jnp.bfloat16):
    level = block_levels(own_key, extent, cuts, -0.22, 0.18) if cuts else 1.0
    result = jax.random.normal(own_key, extent, jnp.float32) * spread * level
    return jnp.minimum(jnp.maximum(result, -reach), reach).astype(held_as)


def setup_inputs(seed: int = 0) -> dict:
    streams_of = jax.random.split(jax.random.key(seed), 7)
    return {
        "query": draw_query(jax.random.fold_in(streams_of[6], 71), 0),
        "key": draw_key(jax.random.fold_in(streams_of[6], 71), 0),
        "value": noise(streams_of[2], (N_PP, SEQ, KVH * HD), 1.0, 6.0, ((0, 4), (1, 4), (2, 2))),
        "out_grad": noise(streams_of[3], (N_PP, SEQ, HEADS * HD), 4.0, 24.0, ((0, 4), (1, 4), (2, 2))),
        "lengths": uneven(streams_of[4], NDOC, SEQ, SEQ // 2, 2).astype(jnp.int32),
        "plan": jax.vmap(lambda own: jax.random.permutation(own, N_CP))(jax.random.split(streams_of[5], N_CP)).reshape((N_CP, N_CP)).astype(jnp.int32),
    }


def doc_table(lengths, count):
    ends = jnp.cumsum(lengths).astype(jnp.int32)
    position = jnp.arange(count, dtype=jnp.int32)
    owner = jnp.sum((position[:, None] >= ends[None, :]).astype(jnp.int32), axis=1)
    return owner, position


def reference(query, key, value, out_grad, lengths, plan):
    sections = query.shape[0]
    length = query.shape[1]
    head_count = query.shape[2] // HD
    kv_count = key.shape[2] // HD
    group = head_count // kv_count
    score_scale = HD ** -0.5
    owner, position = doc_table(lengths, length)
    visible = (owner[:, None] == owner[None, :]) & (position[None, :] <= position[:, None])
    visible_rows = jnp.repeat(visible, group, axis=0)

    def one_head(index):
        section = index // kv_count
        kv_head = index % kv_count
        q_section = lax.dynamic_index_in_dim(query, section, 0, keepdims=False)
        g_section = lax.dynamic_index_in_dim(out_grad, section, 0, keepdims=False)
        k_section = lax.dynamic_index_in_dim(key, section, 0, keepdims=False)
        v_section = lax.dynamic_index_in_dim(value, section, 0, keepdims=False)
        q_rows = lax.dynamic_slice_in_dim(q_section, kv_head * group * HD, group * HD, 1).reshape(length * group, HD)
        g_rows = lax.dynamic_slice_in_dim(g_section, kv_head * group * HD, group * HD, 1).reshape(length * group, HD)
        k_rows = lax.dynamic_slice_in_dim(k_section, kv_head * HD, HD, 1)
        v_rows = lax.dynamic_slice_in_dim(v_section, kv_head * HD, HD, 1)
        scores = jnp.dot(q_rows, k_rows.T, preferred_element_type=jnp.float32) * score_scale
        scores = jnp.where(visible_rows, scores, -jnp.inf)
        top = jnp.max(scores, axis=1, keepdims=True)
        expo = jnp.exp(scores - top)
        probs = expo / jnp.sum(expo, axis=1, keepdims=True)
        dprob = jnp.dot(g_rows, v_rows.T, preferred_element_type=jnp.float32)
        delta = jnp.sum(probs * dprob, axis=1, keepdims=True)
        probs_low = probs.astype(jnp.bfloat16)
        dscore = (probs * (dprob - delta) * score_scale).astype(jnp.bfloat16)
        dvalue = jnp.dot(probs_low.T, g_rows, preferred_element_type=jnp.float32)
        dkey = jnp.dot(dscore.T, q_rows, preferred_element_type=jnp.float32)
        dquery = jnp.dot(dscore, k_rows, preferred_element_type=jnp.float32).astype(jnp.bfloat16)
        return dquery.reshape(length, group * HD), dkey.astype(jnp.bfloat16), dvalue.astype(jnp.bfloat16)

    dquery, dkey, dvalue = lax.map(one_head, jnp.arange(sections * kv_count, dtype=jnp.int32))
    dquery = dquery.reshape(sections, kv_count, length, group * HD).transpose(0, 2, 1, 3).reshape(sections, length, head_count * HD)
    dkey = dkey.reshape(sections, kv_count, length, HD).transpose(0, 2, 1, 3).reshape(sections, length, kv_count * HD)
    dvalue = dvalue.reshape(sections, kv_count, length, HD).transpose(0, 2, 1, 3).reshape(sections, length, kv_count * HD)
    shards = plan.shape[0]
    block_rows = length // (shards * shards)
    iota = jnp.arange(shards, dtype=jnp.int32)
    inverse = jnp.sum((plan[:, None, :] == iota[None, :, None]).astype(jnp.int32) * iota[None, None, :], axis=2).astype(jnp.int32)
    natural = dquery.reshape(sections, shards, shards, block_rows, head_count * HD)
    planned = jnp.take_along_axis(natural, inverse[None, :, :, None, None], axis=2)
    planned = planned.transpose(0, 2, 1, 3, 4).reshape(sections, length, head_count * HD)
    handed = jnp.concatenate([planned[1:], jnp.zeros((1, length, head_count * HD), jnp.bfloat16)], axis=0)
    return handed, dkey, dvalue
```

```python
import functools
import math

import jax
import jax.numpy as jnp
from jax import lax
from jax.experimental import pallas as pl
from jax.experimental.pallas import tpu as pltpu
from jax.sharding import PartitionSpec as P

MESH = pl.DeviceIdType.MESH
F32 = jnp.float32
BF16 = jnp.bfloat16
NT = (((1,), (1,)), ((), ()))


def kernel(
    sizes,
    plan_ref, lens_ref, q_hbm, k_hbm, v_hbm, g_hbm,
    handed, kg_ref, vg_ref,
    qraw, graw, qs, gs, kall, vall, kt, bias, pst, dst, stag, zero, dsend, drecv, acc,
    in_sem, own_sem, kv_send, kv_recv, dq_send, dq_recv, d_send, d_recv, zero_sem,
):
    n_pp, n_cp, tokens, heads, nkv, hd, ndoc, groups, chunk = sizes
    group_heads = heads // nkv
    per_group = n_cp // groups
    block_rows = tokens // n_cp
    me = lax.axis_index("cp")
    sec = lax.axis_index("pp")
    my_group = me // per_group
    scale = hd ** -0.5

    q_in = pltpu.make_async_copy(q_hbm.at[0], qraw, in_sem.at[0])
    g_in = pltpu.make_async_copy(g_hbm.at[0], graw, in_sem.at[1])
    q_in.start()
    g_in.start()
    my_rows = pl.ds(pl.multiple_of(me * tokens, tokens), tokens)
    k_own = pltpu.make_async_copy(k_hbm.at[0], kall.at[my_rows], own_sem.at[0])
    v_own = pltpu.make_async_copy(v_hbm.at[0], vall.at[my_rows], own_sem.at[1])
    k_own.start()
    v_own.start()

    barrier = pltpu.get_barrier_semaphore()
    for d in range(n_cp):
        @pl.when(me != d)
        def _():
            pl.semaphore_signal(barrier, inc=1, device_id={"cp": d}, device_id_type=MESH)

        @pl.when(sec < n_pp - 1)
        def _():
            pl.semaphore_signal(barrier, inc=1, device_id={"pp": sec + 1, "cp": d}, device_id_type=MESH)

    @pl.when(sec > 0)
    def _():
        pl.semaphore_wait(barrier, 2 * n_cp - 1)

    @pl.when(sec == 0)
    def _():
        pl.semaphore_wait(barrier, n_cp - 1)

    def kv_copies(d, source):
        rows = pl.ds(pl.multiple_of(source * tokens, tokens), tokens)
        return [
            pltpu.make_async_remote_copy(
                src_ref=hbm.at[0], dst_ref=full.at[rows],
                send_sem=kv_send.at[i, d], recv_sem=kv_recv.at[i, source],
                device_id={"cp": d}, device_id_type=MESH,
            )
            for i, (hbm, full) in enumerate(((k_hbm, kall), (v_hbm, vall)))
        ]

    for d in reversed(range(n_cp)):
        @pl.when((me != d) & (my_group <= d // per_group))
        def _():
            for copy in kv_copies(d, me):
                copy.start()

    @pl.when(sec == n_pp - 1)
    def _():
        zero[...] = jnp.zeros_like(zero)
        pltpu.make_async_copy(zero, handed.at[0], zero_sem).start()

    def taken_of(slot):
        taken = jnp.zeros_like(slot)
        for d in range(n_cp):
            inverse = jnp.int32(0)
            for j in range(1, n_cp):
                inverse = inverse + jnp.where(plan_ref[me, j] == d, j, 0)
            taken = jnp.where(slot == d, inverse, taken)
        return taken

    row = lax.broadcasted_iota(jnp.int32, (tokens, tokens), 0)
    col = lax.broadcasted_iota(jnp.int32, (tokens, tokens), 1)
    row_slot = row // block_rows
    local = taken_of(row_slot) * block_rows + (row - row_slot * block_rows)
    perm = jnp.where(local == col, 1.0, 0.0).astype(BF16)

    lane = lax.broadcasted_iota(jnp.int32, (1, tokens), 1)
    lane_slot = lane // block_rows
    q_pos = me * tokens + taken_of(lane_slot) * block_rows + (lane - lane_slot * block_rows)
    begin = jnp.zeros_like(q_pos)
    end = jnp.int32(0)
    for i in range(ndoc):
        end = end + lens_ref[i]
        begin = jnp.where(q_pos >= end, end, begin)
    for s in range(n_cp):
        k_pos = lax.broadcasted_iota(jnp.int32, (tokens, tokens), 0) + s * tokens
        seen = (k_pos >= begin) & (k_pos <= q_pos)
        bias[s * tokens:(s + 1) * tokens, :] = jnp.where(seen, 0.0, -jnp.inf)

    q_in.wait()
    g_in.wait()

    def stack(raw, out, c):
        width = 4 * hd
        cols = pl.ds(pl.multiple_of(c * width, width), width)
        moved = jnp.dot(perm, raw[:, cols], preferred_element_type=F32).astype(BF16)
        for h in range(4):
            at = pl.ds(pl.multiple_of((c * 4 + h) * tokens, tokens), tokens)
            out[at, :] = moved[:, h * hd:(h + 1) * hd]

    def stack_both(c, carry):
        stack(qraw, qs, c)
        stack(graw, gs, c)
        return carry

    lax.fori_loop(0, heads // 4, stack_both, 0)
    k_own.wait()
    v_own.wait()

    def dq_copy(d, cols):
        return pltpu.make_async_remote_copy(
            src_ref=stag.at[pl.ds(d * block_rows, block_rows), cols],
            dst_ref=handed.at[0, pl.ds(pl.multiple_of(me * block_rows, block_rows), block_rows), cols],
            send_sem=dq_send, recv_sem=dq_recv,
            device_id={"pp": sec - 1, "cp": d}, device_id_type=MESH,
        )

    def d_copy(kb, source, cols):
        at = pl.ds(pl.multiple_of(source * tokens, tokens), tokens)
        return pltpu.make_async_remote_copy(
            src_ref=dsend.at[pl.ds(kb * tokens, tokens), cols],
            dst_ref=drecv.at[at, cols],
            send_sem=d_send.at[kb], recv_sem=d_recv.at[source],
            device_id={"cp": kb}, device_id_type=MESH,
        )

    def work(group):
        shards = (group + 1) * per_group
        count = shards * tokens
        for s in range(shards):
            @pl.when(me != s)
            def _():
                for copy in kv_copies(s, s):
                    copy.wait_recv()

        def one_kv(kv, carry):
            kv_cols = pl.ds(pl.multiple_of(kv * hd, hd), hd)
            for s in range(shards):
                at = slice(s * tokens, (s + 1) * tokens)
                kt[:, at] = kall[at, kv_cols].astype(F32).T.astype(BF16)

            def one_chunk(c, carry):
                for pair in range(chunk // 2):
                    first = c * chunk + pair * 2
                    rows = pl.ds(pl.multiple_of((kv * group_heads + first) * tokens, 2 * tokens), 2 * tokens)
                    kept = pl.ds(pl.multiple_of(first * tokens, 2 * tokens), 2 * tokens)
                    seen = bias[0:count, :]
                    score = lax.dot_general(kall[0:count, kv_cols], qs[rows, :], NT, preferred_element_type=F32)
                    score = score + jnp.concatenate([seen, seen], axis=1)
                    dprob = lax.dot_general(vall[0:count, kv_cols], gs[rows, :], NT, preferred_element_type=F32)
                    top = jnp.max(score, axis=0, keepdims=True)
                    expo = jnp.exp2((score - top) * (scale * math.log2(math.e)))
                    inverse = 1.0 / jnp.sum(expo, axis=0, keepdims=True)
                    delta = jnp.sum(expo * dprob, axis=0, keepdims=True) * inverse
                    pst[0:count, kept] = (expo * inverse).astype(BF16)
                    dscore = (expo * (inverse * scale) * (dprob - delta)).astype(BF16)
                    dst[0:count, kept] = dscore

                    @pl.when(sec > 0)
                    def _():
                        dqt = jnp.dot(kt[:, 0:count], dscore, preferred_element_type=F32)
                        for h in range(2):
                            at = pl.ds(pl.multiple_of((kv * group_heads + first + h) * hd, hd), hd)
                            stag[:, at] = dqt[:, h * tokens:(h + 1) * tokens].T.astype(stag.dtype)

                @pl.when(sec > 0)
                def _():
                    width = chunk * hd
                    cols = pl.ds(pl.multiple_of(kv * group_heads * hd + c * width, width), width)
                    for d in range(n_cp):
                        dq_copy(d, cols).start()

                return carry

            lax.fori_loop(0, group_heads // chunk, one_chunk, 0)

            all_rows = pl.ds(pl.multiple_of(kv * group_heads * tokens, group_heads * tokens), group_heads * tokens)
            term_cols = pl.ds(pl.multiple_of(kv * 2 * hd, 2 * hd), 2 * hd)
            for kb in range(shards):
                at = slice(kb * tokens, (kb + 1) * tokens)
                dkey = jnp.dot(dst[at, :], qs[all_rows, :], preferred_element_type=F32)
                dvalue = jnp.dot(pst[at, :], gs[all_rows, :], preferred_element_type=F32)
                both = jnp.concatenate([dkey, dvalue], axis=1)

                @pl.when(me == kb)
                def _():
                    acc[:, term_cols] = both

                @pl.when(me != kb)
                def _():
                    dsend[at, term_cols] = both.astype(BF16)
                    d_copy(kb, me, term_cols).start()

            return carry

        if nkv == 1:
            one_kv(0, 0)
        else:
            lax.fori_loop(0, nkv, one_kv, 0)

    for group in range(groups):
        pl.when(my_group == group)(functools.partial(work, group))

    everything = pl.ds(0, nkv * 2 * hd)
    for s in range(n_cp):
        @pl.when((me != s) & (my_group <= s // per_group))
        def _():
            d_copy(0, s, everything).wait_recv()
            acc[...] += drecv[s * tokens:(s + 1) * tokens, :].astype(F32)

    for kv in range(nkv):
        kg_ref[0, :, kv * hd:(kv + 1) * hd] = acc[:, kv * 2 * hd:kv * 2 * hd + hd].astype(BF16)
        vg_ref[0, :, kv * hd:(kv + 1) * hd] = acc[:, kv * 2 * hd + hd:(kv + 1) * 2 * hd].astype(BF16)

    for d in range(n_cp):
        @pl.when((me != d) & (my_group <= d // per_group))
        def _():
            for copy in kv_copies(d, me):
                copy.wait_send()

        @pl.when((me != d) & (my_group >= d // per_group))
        def _():
            d_copy(d, me, everything).wait_send()

    whole = pltpu.make_async_remote_copy(
        src_ref=stag, dst_ref=handed.at[0], send_sem=dq_send, recv_sem=dq_recv,
        device_id={"pp": lax.rem(sec + 1, n_pp)}, device_id_type=MESH,
    )

    @pl.when(sec > 0)
    def _():
        whole.wait_send()

    @pl.when(sec < n_pp - 1)
    def _():
        whole.wait_recv()

    @pl.when(sec == n_pp - 1)
    def _():
        pltpu.make_async_copy(zero, handed.at[0], zero_sem).wait()


def body(n_pp, n_cp, n_tp, query, key, value, out_grad, lengths, plan):
    tokens, width = query.shape[1], query.shape[2]
    kv_width = key.shape[2]
    hd = 128
    heads, nkv = width // hd, kv_width // hd
    groups = min(n_cp, 4)
    block_rows = tokens // n_cp
    seq = n_cp * tokens
    wide = BF16 if block_rows % 16 == 0 else F32
    chunk = 4
    group_rows = heads // nkv * tokens
    sizes = (n_pp, n_cp, tokens, heads, nkv, hd, lengths.shape[0], groups, chunk)
    anywhere = pl.BlockSpec(memory_space=pl.ANY)
    vmem = pl.BlockSpec(memory_space=pltpu.VMEM)
    smem = pl.BlockSpec(memory_space=pltpu.SMEM)
    dma = pltpu.SemaphoreType.DMA
    handed, key_grad, value_grad = pl.pallas_call(
        functools.partial(kernel, sizes),
        out_shape=(
            jax.ShapeDtypeStruct(query.shape, wide),
            jax.ShapeDtypeStruct(key.shape, BF16),
            jax.ShapeDtypeStruct(value.shape, BF16),
        ),
        in_specs=[smem, smem, anywhere, anywhere, anywhere, anywhere],
        out_specs=(anywhere, vmem, vmem),
        scratch_shapes=[
            pltpu.VMEM((tokens, width), BF16),
            pltpu.VMEM((tokens, width), BF16),
            pltpu.VMEM((heads * tokens, hd), BF16),
            pltpu.VMEM((heads * tokens, hd), BF16),
            pltpu.VMEM((seq, kv_width), BF16),
            pltpu.VMEM((seq, kv_width), BF16),
            pltpu.VMEM((hd, seq), BF16),
            pltpu.VMEM((seq, tokens), F32),
            pltpu.VMEM((seq, group_rows), BF16),
            pltpu.VMEM((seq, group_rows), BF16),
            pltpu.VMEM((tokens, width), wide),
            pltpu.VMEM((tokens, width), wide),
            pltpu.VMEM((seq, 2 * kv_width), BF16),
            pltpu.VMEM((seq, 2 * kv_width), BF16),
            pltpu.VMEM((tokens, 2 * kv_width), F32),
            dma((2,)), dma((2,)), dma((2, n_cp)), dma((2, n_cp)),
            dma, dma, dma((n_cp,)), dma((n_cp,)), dma,
        ],
        compiler_params=pltpu.CompilerParams(
            collective_id=0, has_side_effects=True, vmem_limit_bytes=(56 if seq > 512 else 32) * 2 ** 20
        ),
        cost_estimate=pl.CostEstimate(
            flops=10 * tokens * heads * seq * hd, bytes_accessed=6 * tokens * width,
            transcendentals=tokens * heads * seq,
        ),
    )(plan, lengths, query, key, value, out_grad)
    return handed.astype(BF16), key_grad, value_grad


def solution(mesh):
    spec = P("pp", "cp", "tp")
    sizes = (mesh.shape["pp"], mesh.shape["cp"], mesh.shape["tp"])
    return jax.shard_map(
        functools.partial(body, *sizes),
        mesh=mesh,
        in_specs=(spec, spec, spec, spec, P(), P()),
        out_specs=(spec, spec, spec),
        check_vma=False,
    )
```

```python
import functools
import math

import jax
import jax.numpy as jnp
from jax import lax
from jax.experimental import pallas as pl
from jax.experimental.pallas import tpu as pltpu
from jax.sharding import PartitionSpec as P

MESH = pl.DeviceIdType.MESH
F32 = jnp.float32
BF16 = jnp.bfloat16
VMEM = 60 * 2 ** 20
NT = (((1,), (1,)), ((), ()))


def kernel(
    sizes,
    plan_hbm, lens_hbm, q_hbm, k_hbm, v_hbm, g_hbm,
    handed, kg_ref, vg_ref,
    plan_ref, lens_ref, qraw, graw, qs, gs, kall, vall, kt, bias, pst, dst, stag, zero, term, dsend, drecv,
    in_sem, own_sem, kv_send, kv_recv, dq_send, dq_recv, d_send, d_recv, zero_sem, table_sem,
):
    n_pp, n_cp, tokens, heads, nkv, hd, ndoc, groups, chunk = sizes
    group_heads = heads // nkv
    per_group = n_cp // groups
    block_rows = tokens // n_cp
    me = lax.axis_index("cp")
    sec = lax.axis_index("pp")
    my_group = me // per_group
    scale = hd ** -0.5

    barrier = pltpu.get_barrier_semaphore()

    @pl.when(me > 0)
    def _():
        pl.semaphore_signal(barrier, inc=1, device_id={"cp": me - 1}, device_id_type=MESH)

    @pl.when(me < n_cp - 1)
    def _():
        pl.semaphore_signal(barrier, inc=1, device_id={"cp": me + 1}, device_id_type=MESH)

    @pl.when(sec < n_pp - 1)
    def _():
        for d in range(n_cp):
            pl.semaphore_signal(barrier, inc=1, device_id={"pp": sec + 1, "cp": d}, device_id_type=MESH)

    plan_in = pltpu.make_async_copy(plan_hbm, plan_ref, table_sem.at[0])
    lens_in = pltpu.make_async_copy(lens_hbm, lens_ref, table_sem.at[1])
    my_rows = pl.ds(pl.multiple_of(me * tokens, tokens), tokens)
    k_own = pltpu.make_async_copy(k_hbm.at[0], kall.at[my_rows], own_sem.at[0])
    v_own = pltpu.make_async_copy(v_hbm.at[0], vall.at[my_rows], own_sem.at[1])
    q_in = pltpu.make_async_copy(q_hbm.at[0], qraw, in_sem.at[0])
    g_in = pltpu.make_async_copy(g_hbm.at[0], graw, in_sem.at[1])
    for copy in (plan_in, lens_in, k_own, v_own, q_in, g_in):
        copy.start()

    neighbours = jnp.where(me > 0, 1, 0) + jnp.where(me < n_cp - 1, 1, 0)
    pl.semaphore_wait(barrier, neighbours + jnp.where(sec > 0, n_cp, 0))

    def kv_copies(source, own):
        rows = pl.ds(pl.multiple_of(source * tokens, tokens), tokens)
        return [
            pltpu.make_async_remote_copy(
                src_ref=hbm.at[0] if own else full.at[rows], dst_ref=full.at[rows],
                send_sem=kv_send.at[i, source], recv_sem=kv_recv.at[i, source],
                device_id={"cp": lax.rem(me + 1, n_cp)}, device_id_type=MESH,
            )
            for i, (hbm, full) in enumerate(((k_hbm, kall), (v_hbm, vall)))
        ]

    @pl.when(me < n_cp - 1)
    def _():
        for copy in kv_copies(me, True):
            copy.start()

    @pl.when(sec == n_pp - 1)
    def _():
        zero[...] = jnp.zeros_like(zero)
        for d in range(n_cp):
            pltpu.make_async_copy(zero, handed.at[0, pl.ds(d * block_rows, block_rows)], zero_sem).start()

    plan_in.wait()
    lens_in.wait()

    def taken_of(slot):
        taken = jnp.zeros_like(slot)
        for d in range(n_cp):
            inverse = jnp.int32(0)
            for j in range(1, n_cp):
                inverse = inverse + jnp.where(plan_ref[me, j] == d, j, 0)
            taken = jnp.where(slot == d, inverse, taken)
        return taken

    row = lax.broadcasted_iota(jnp.int32, (tokens, tokens), 0)
    col = lax.broadcasted_iota(jnp.int32, (tokens, tokens), 1)
    row_slot = row // block_rows
    local = taken_of(row_slot) * block_rows + (row - row_slot * block_rows)
    perm = jnp.where(local == col, 1.0, 0.0).astype(BF16)

    lane = lax.broadcasted_iota(jnp.int32, (1, tokens), 1)
    lane_slot = lane // block_rows
    q_pos = me * tokens + taken_of(lane_slot) * block_rows + (lane - lane_slot * block_rows)
    begin = jnp.zeros_like(q_pos)
    end = jnp.int32(0)
    for i in range(ndoc):
        end = end + lens_ref[i]
        begin = jnp.where(q_pos >= end, end, begin)
    for s in range(n_cp):
        k_pos = lax.broadcasted_iota(jnp.int32, (tokens, tokens), 0) + s * tokens
        seen = (k_pos >= begin) & (k_pos <= q_pos)
        bias[s * tokens:(s + 1) * tokens, :] = jnp.where(seen, 0.0, -jnp.inf)

    q_in.wait()
    g_in.wait()

    def stack(raw, out, c):
        width = 4 * hd
        cols = pl.ds(pl.multiple_of(c * width, width), width)
        moved = jnp.dot(perm, raw[:, cols], preferred_element_type=F32).astype(BF16)
        for h in range(4):
            at = pl.ds(pl.multiple_of((c * 4 + h) * tokens, tokens), tokens)
            out[at, :] = moved[:, h * hd:(h + 1) * hd]

    def stack_both(c, carry):
        stack(qraw, qs, c)
        stack(graw, gs, c)
        return carry

    lax.fori_loop(0, heads // 4, stack_both, 0)
    k_own.wait()
    v_own.wait()

    def dq_copy(d, cols):
        return pltpu.make_async_remote_copy(
            src_ref=stag.at[pl.ds(d * block_rows, block_rows), cols],
            dst_ref=handed.at[0, pl.ds(pl.multiple_of(me * block_rows, block_rows), block_rows), cols],
            send_sem=dq_send, recv_sem=dq_recv,
            device_id={"pp": sec - 1, "cp": d}, device_id_type=MESH,
        )

    def d_copy(kb, kv, cols):
        at = pl.ds(kb * tokens, tokens)
        source = term if drecv.dtype == F32 else dsend
        return pltpu.make_async_remote_copy(
            src_ref=source.at[at, cols], dst_ref=drecv.at[at, cols],
            send_sem=d_send.at[kb, kv], recv_sem=d_recv.at[kb, kv],
            device_id={"cp": lax.rem(me + n_cp - 1, n_cp)}, device_id_type=MESH,
        )

    for off in range(1, n_cp):
        @pl.when(me >= off)
        def _():
            for copy in kv_copies(me - off, False):
                copy.wait_recv()

            @pl.when(me < n_cp - 1)
            def _():
                for copy in kv_copies(me - off, False):
                    copy.start()

    def work(group):
        shards = (group + 1) * per_group
        count = shards * tokens
        for s in range(group * per_group + 1, shards):
            @pl.when(me < s)
            def _():
                kall[s * tokens:(s + 1) * tokens, :] = jnp.zeros((tokens, kall.shape[1]), BF16)
                vall[s * tokens:(s + 1) * tokens, :] = jnp.zeros((tokens, vall.shape[1]), BF16)

        def one_kv(kv, carry):
            kv_cols = pl.ds(pl.multiple_of(kv * hd, hd), hd)
            for s in range(shards):
                at = slice(s * tokens, (s + 1) * tokens)
                kt[:, at] = kall[at, kv_cols].astype(F32).T.astype(BF16)

            def one_chunk(c, carry):
                for pair in range(chunk // 2):
                    first = c * chunk + pair * 2
                    rows = pl.ds(pl.multiple_of((kv * group_heads + first) * tokens, 2 * tokens), 2 * tokens)
                    kept = pl.ds(pl.multiple_of(first * tokens, 2 * tokens), 2 * tokens)
                    seen = bias[0:count, :]
                    score = lax.dot_general(kall[0:count, kv_cols], qs[rows, :], NT, preferred_element_type=F32)
                    score = score + jnp.concatenate([seen, seen], axis=1)
                    dprob = lax.dot_general(vall[0:count, kv_cols], gs[rows, :], NT, preferred_element_type=F32)
                    top = jnp.max(score, axis=0, keepdims=True)
                    expo = jnp.exp2((score - top) * (scale * math.log2(math.e)))
                    inverse = 1.0 / jnp.sum(expo, axis=0, keepdims=True)
                    delta = jnp.sum(expo * dprob, axis=0, keepdims=True) * inverse
                    pst[0:count, kept] = (expo * inverse).astype(BF16)
                    dscore = (expo * (inverse * scale) * (dprob - delta)).astype(BF16)
                    dst[0:count, kept] = dscore

                    @pl.when(sec > 0)
                    def _():
                        dqt = jnp.dot(kt[:, 0:count], dscore, preferred_element_type=F32)
                        for h in range(2):
                            at = pl.ds(pl.multiple_of((kv * group_heads + first + h) * hd, hd), hd)
                            stag[:, at] = dqt[:, h * tokens:(h + 1) * tokens].T.astype(stag.dtype)

                @pl.when(sec > 0)
                def _():
                    width = chunk * hd
                    cols = pl.ds(pl.multiple_of(kv * group_heads * hd + c * width, width), width)
                    for d in range(n_cp):
                        dq_copy(d, cols).start()

                return carry

            lax.fori_loop(0, group_heads // chunk, one_chunk, 0)

            all_rows = pl.ds(pl.multiple_of(kv * group_heads * tokens, group_heads * tokens), group_heads * tokens)
            term_cols = pl.ds(pl.multiple_of(kv * 2 * hd, 2 * hd), 2 * hd)
            for kb in range(shards):
                at = slice(kb * tokens, (kb + 1) * tokens)
                dkey = jnp.dot(dst[at, :], qs[all_rows, :], preferred_element_type=F32)
                dvalue = jnp.dot(pst[at, :], gs[all_rows, :], preferred_element_type=F32)
                term[at, term_cols] = jnp.concatenate([dkey, dvalue], axis=1)

            for kb in range(shards):
                at = slice(kb * tokens, (kb + 1) * tokens)

                @pl.when((kb <= me) & (me < n_cp - 1))
                def _():
                    d_copy(kb, kv, term_cols).wait_recv()
                    term[at, term_cols] += drecv[at, term_cols].astype(F32)

                @pl.when(kb < me)
                def _():
                    if drecv.dtype != F32:
                        dsend[at, term_cols] = term[at, term_cols].astype(BF16)
                    d_copy(kb, kv, term_cols).start()

            return carry

        if nkv == 1:
            one_kv(0, 0)
        else:
            lax.fori_loop(0, nkv, one_kv, 0)

    for group in range(groups):
        pl.when(my_group == group)(functools.partial(work, group))

    for kv in range(nkv):
        at = kv * 2 * hd
        kg_ref[0, :, kv * hd:(kv + 1) * hd] = term[my_rows, at:at + hd].astype(BF16)
        vg_ref[0, :, kv * hd:(kv + 1) * hd] = term[my_rows, at + hd:at + 2 * hd].astype(BF16)

    @pl.when(me < n_cp - 1)
    def _():
        for copy in kv_copies(me, True):
            copy.wait_send()

    for s in range(n_cp - 1):
        @pl.when((s < me) & (me < n_cp - 1))
        def _():
            for copy in kv_copies(s, False):
                copy.wait_send()

        @pl.when(s < me)
        def _():
            for kv in range(nkv):
                d_copy(s, kv, pl.ds(kv * 2 * hd, 2 * hd)).wait_send()

    whole = pltpu.make_async_remote_copy(
        src_ref=stag, dst_ref=handed.at[0], send_sem=dq_send, recv_sem=dq_recv,
        device_id={"pp": lax.rem(sec + 1, n_pp)}, device_id_type=MESH,
    )

    @pl.when(sec > 0)
    def _():
        whole.wait_send()

    @pl.when(sec < n_pp - 1)
    def _():
        whole.wait_recv()

    @pl.when(sec == n_pp - 1)
    def _():
        pltpu.make_async_copy(stag, handed.at[0], zero_sem).wait()


def finish(handed, kg, vg, handed_out, kg_out, vg_out, sem):
    pairs = ((handed, handed_out), (kg, kg_out), (vg, vg_out))
    copies = [pltpu.make_async_copy(a, b, sem.at[i]) for i, (a, b) in enumerate(pairs)]
    for copy in copies:
        copy.start()
    for copy in copies:
        copy.wait()


def body(n_pp, n_cp, n_tp, query, key, value, out_grad, lengths, plan):
    tokens, width = query.shape[1], query.shape[2]
    kv_width = key.shape[2]
    hd = 128
    heads, nkv = width // hd, kv_width // hd
    groups = min(n_cp, 4)
    block_rows = tokens // n_cp
    seq = n_cp * tokens
    wide = BF16 if block_rows % 16 == 0 else F32
    chunk = 4
    group_rows = heads // nkv * tokens
    sizes = (n_pp, n_cp, tokens, heads, nkv, hd, lengths.shape[0], groups, chunk)
    hop = BF16 if n_cp <= 4 else F32
    hbm = pl.BlockSpec(memory_space=pltpu.HBM)
    anywhere = pl.BlockSpec(memory_space=pl.ANY)
    vmem = pl.BlockSpec(memory_space=pltpu.VMEM)
    dma = pltpu.SemaphoreType.DMA
    handed, key_grad, value_grad = pl.pallas_call(
        functools.partial(kernel, sizes),
        out_shape=(
            jax.ShapeDtypeStruct(query.shape, wide),
            jax.ShapeDtypeStruct(key.shape, BF16),
            jax.ShapeDtypeStruct(value.shape, BF16),
        ),
        in_specs=[hbm] * 6,
        out_specs=(anywhere, vmem, vmem),
        scratch_shapes=[
            pltpu.SMEM(plan.shape, jnp.int32),
            pltpu.SMEM(lengths.shape, jnp.int32),
            pltpu.VMEM((tokens, width), BF16),
            pltpu.VMEM((tokens, width), BF16),
            pltpu.VMEM((heads * tokens, hd), BF16),
            pltpu.VMEM((heads * tokens, hd), BF16),
            pltpu.VMEM((seq, kv_width), BF16),
            pltpu.VMEM((seq, kv_width), BF16),
            pltpu.VMEM((hd, seq), BF16),
            pltpu.VMEM((seq, tokens), F32),
            pltpu.VMEM((seq, group_rows), BF16),
            pltpu.VMEM((seq, group_rows), BF16),
            pltpu.VMEM((tokens, width), wide),
            pltpu.VMEM((block_rows, width), wide),
            pltpu.VMEM((seq, 2 * kv_width), F32),
            pltpu.VMEM((seq, 2 * kv_width) if hop == BF16 else (16, 128), BF16),
            pltpu.VMEM((seq, 2 * kv_width), hop),
            dma((2,)), dma((2,)), dma((2, n_cp)), dma((2, n_cp)),
            dma, dma, dma((n_cp, nkv)), dma((n_cp, nkv)), dma, dma((2,)),
        ],
        compiler_params=pltpu.CompilerParams(
            collective_id=0, has_side_effects=True, vmem_limit_bytes=VMEM
        ),
        cost_estimate=pl.CostEstimate(
            flops=10 * tokens * heads * seq * hd, bytes_accessed=6 * tokens * width,
            transcendentals=tokens * heads * seq,
        ),
    )(plan, lengths, query, key, value, out_grad)
    if wide != BF16:
        return handed.astype(BF16), key_grad, value_grad
    results = (handed, key_grad, value_grad)
    return pl.pallas_call(
        finish,
        out_shape=tuple(jax.ShapeDtypeStruct(r.shape, r.dtype) for r in results),
        in_specs=[anywhere] * 3,
        out_specs=(hbm,) * 3,
        scratch_shapes=[dma((3,))],
        compiler_params=pltpu.CompilerParams(vmem_limit_bytes=VMEM),
    )(*results)


def solution(mesh):
    spec = P("pp", "cp", "tp")
    sizes = (mesh.shape["pp"], mesh.shape["cp"], mesh.shape["tp"])
    return jax.shard_map(
        functools.partial(body, *sizes),
        mesh=mesh,
        in_specs=(spec, spec, spec, spec, P(), P()),
        out_specs=(spec, spec, spec),
        check_vma=False,
    )
```

```python
import functools
import math

import jax
import jax.numpy as jnp
from jax import lax
from jax.experimental import pallas as pl
from jax.experimental.pallas import tpu as pltpu
from jax.sharding import PartitionSpec as P

MESH = pl.DeviceIdType.MESH
F32 = jnp.float32
BF16 = jnp.bfloat16
VMEM = 60 * 2 ** 20
NT = (((1,), (1,)), ((), ()))


def kernel(
    sizes,
    plan_hbm, lens_hbm, q_hbm, k_hbm, v_hbm, g_hbm,
    handed, kg_ref, vg_ref,
    plan_ref, lens_ref, qraw, graw, qs, gs, kall, vall, kt, bias, pst, dst, stag, land, acc, dsend, drecv,
    in_sem, own_sem, kv_send, kv_recv, dq_send, dq_recv, d_send, d_recv, out_sem, table_sem,
):
    n_pp, n_cp, tokens, heads, nkv, hd, ndoc, groups, chunk = sizes
    group_heads = heads // nkv
    per_group = n_cp // groups
    block_rows = tokens // n_cp
    me = lax.axis_index("cp")
    sec = lax.axis_index("pp")
    my_group = me // per_group
    scale = hd ** -0.5

    barrier = pltpu.get_barrier_semaphore()

    for d in range(n_cp):
        @pl.when(me != d)
        def _():
            pl.semaphore_signal(barrier, inc=1, device_id={"cp": d}, device_id_type=MESH)

    @pl.when(sec < n_pp - 1)
    def _():
        for d in range(n_cp):
            pl.semaphore_signal(barrier, inc=1, device_id={"pp": sec + 1, "cp": d}, device_id_type=MESH)

    plan_in = pltpu.make_async_copy(plan_hbm, plan_ref, table_sem.at[0])
    lens_in = pltpu.make_async_copy(lens_hbm, lens_ref, table_sem.at[1])
    my_rows = pl.ds(pl.multiple_of(me * tokens, tokens), tokens)
    k_own = pltpu.make_async_copy(k_hbm.at[0], kall.at[my_rows], own_sem.at[0])
    v_own = pltpu.make_async_copy(v_hbm.at[0], vall.at[my_rows], own_sem.at[1])
    q_in = pltpu.make_async_copy(q_hbm.at[0], qraw, in_sem.at[0])
    g_in = pltpu.make_async_copy(g_hbm.at[0], graw, in_sem.at[1])
    for copy in (plan_in, lens_in, k_own, v_own, q_in, g_in):
        copy.start()

    pl.semaphore_wait(barrier, n_cp - 1 + jnp.where(sec > 0, n_cp, 0))

    def kv_copies(d, source):
        rows = pl.ds(pl.multiple_of(source * tokens, tokens), tokens)
        return [
            pltpu.make_async_remote_copy(
                src_ref=hbm.at[0], dst_ref=full.at[rows],
                send_sem=kv_send.at[i, d], recv_sem=kv_recv.at[i, source],
                device_id={"cp": d}, device_id_type=MESH,
            )
            for i, (hbm, full) in enumerate(((k_hbm, kall), (v_hbm, vall)))
        ]

    for d in reversed(range(n_cp)):
        @pl.when((me != d) & (my_group <= d // per_group))
        def _():
            for copy in kv_copies(d, me):
                copy.start()

    @pl.when(sec == n_pp - 1)
    def _():
        land[...] = jnp.zeros_like(land)

    plan_in.wait()
    lens_in.wait()

    def taken_of(slot):
        taken = jnp.zeros_like(slot)
        for d in range(n_cp):
            inverse = jnp.int32(0)
            for j in range(1, n_cp):
                inverse = inverse + jnp.where(plan_ref[me, j] == d, j, 0)
            taken = jnp.where(slot == d, inverse, taken)
        return taken

    row = lax.broadcasted_iota(jnp.int32, (tokens, tokens), 0)
    col = lax.broadcasted_iota(jnp.int32, (tokens, tokens), 1)
    row_slot = row // block_rows
    local = taken_of(row_slot) * block_rows + (row - row_slot * block_rows)
    perm = jnp.where(local == col, 1.0, 0.0).astype(BF16)

    lane = lax.broadcasted_iota(jnp.int32, (1, tokens), 1)
    lane_slot = lane // block_rows
    q_pos = me * tokens + taken_of(lane_slot) * block_rows + (lane - lane_slot * block_rows)
    begin = jnp.zeros_like(q_pos)
    end = jnp.int32(0)
    for i in range(ndoc):
        end = end + lens_ref[i]
        begin = jnp.where(q_pos >= end, end, begin)
    for s in range(n_cp):
        k_pos = lax.broadcasted_iota(jnp.int32, (tokens, tokens), 0) + s * tokens
        seen = (k_pos >= begin) & (k_pos <= q_pos)
        bias[s * tokens:(s + 1) * tokens, :] = jnp.where(seen, 0.0, -jnp.inf)

    q_in.wait()
    g_in.wait()

    def stack(raw, out, c):
        width = 4 * hd
        cols = pl.ds(pl.multiple_of(c * width, width), width)
        moved = jnp.dot(perm, raw[:, cols], preferred_element_type=F32).astype(BF16)
        for h in range(4):
            at = pl.ds(pl.multiple_of((c * 4 + h) * tokens, tokens), tokens)
            out[at, :] = moved[:, h * hd:(h + 1) * hd]

    def stack_both(c, carry):
        stack(qraw, qs, c)
        stack(graw, gs, c)
        return carry

    lax.fori_loop(0, heads // 4, stack_both, 0)
    k_own.wait()
    v_own.wait()

    def dq_copy(d, piece):
        return pltpu.make_async_remote_copy(
            src_ref=stag.at[piece, pl.ds(d * block_rows, block_rows)],
            dst_ref=land.at[piece, pl.ds(pl.multiple_of(me * block_rows, block_rows), block_rows)],
            send_sem=dq_send, recv_sem=dq_recv.at[piece],
            device_id={"pp": lax.rem(sec + n_pp - 1, n_pp), "cp": d}, device_id_type=MESH,
        )

    def d_copy(kb, source, cols):
        at = pl.ds(pl.multiple_of(source * tokens, tokens), tokens)
        return pltpu.make_async_remote_copy(
            src_ref=dsend.at[pl.ds(kb * tokens, tokens), cols],
            dst_ref=drecv.at[at, cols],
            send_sem=d_send.at[kb], recv_sem=d_recv.at[source],
            device_id={"cp": kb}, device_id_type=MESH,
        )

    def work(group):
        shards = (group + 1) * per_group
        count = shards * tokens
        for s in range(shards):
            @pl.when(me != s)
            def _():
                for copy in kv_copies(s, s):
                    copy.wait_recv()

        def one_kv(kv, carry):
            kv_cols = pl.ds(pl.multiple_of(kv * hd, hd), hd)
            for s in range(shards):
                at = slice(s * tokens, (s + 1) * tokens)
                kt[:, at] = kall[at, kv_cols].astype(F32).T.astype(BF16)

            def one_chunk(c, carry):
                for pair in range(chunk // 2):
                    first = c * chunk + pair * 2
                    rows = pl.ds(pl.multiple_of((kv * group_heads + first) * tokens, 2 * tokens), 2 * tokens)
                    kept = pl.ds(pl.multiple_of(first * tokens, 2 * tokens), 2 * tokens)
                    seen = bias[0:count, :]
                    score = lax.dot_general(kall[0:count, kv_cols], qs[rows, :], NT, preferred_element_type=F32)
                    score = score + jnp.concatenate([seen, seen], axis=1)
                    dprob = lax.dot_general(vall[0:count, kv_cols], gs[rows, :], NT, preferred_element_type=F32)
                    top = jnp.max(score, axis=0, keepdims=True)
                    expo = jnp.exp2((score - top) * (scale * math.log2(math.e)))
                    inverse = 1.0 / jnp.sum(expo, axis=0, keepdims=True)
                    delta = jnp.sum(expo * dprob, axis=0, keepdims=True) * inverse
                    pst[0:count, kept] = (expo * inverse).astype(BF16)
                    dscore = (expo * (inverse * scale) * (dprob - delta)).astype(BF16)
                    dst[0:count, kept] = dscore

                    @pl.when(sec > 0)
                    def _():
                        dqt = jnp.dot(kt[:, 0:count], dscore, preferred_element_type=F32)
                        for h in range(2):
                            at = slice((pair * 2 + h) * hd, (pair * 2 + h + 1) * hd)
                            stag[kv * (group_heads // chunk) + c, :, at] = dqt[:, h * tokens:(h + 1) * tokens].T.astype(stag.dtype)

                @pl.when(sec > 0)
                def _():
                    for d in range(n_cp):
                        dq_copy(d, kv * (group_heads // chunk) + c).start()

                return carry

            lax.fori_loop(0, group_heads // chunk, one_chunk, 0)

            all_rows = pl.ds(pl.multiple_of(kv * group_heads * tokens, group_heads * tokens), group_heads * tokens)
            term_cols = pl.ds(pl.multiple_of(kv * 2 * hd, 2 * hd), 2 * hd)
            for kb in range(shards):
                at = slice(kb * tokens, (kb + 1) * tokens)
                dkey = jnp.dot(dst[at, :], qs[all_rows, :], preferred_element_type=F32)
                dvalue = jnp.dot(pst[at, :], gs[all_rows, :], preferred_element_type=F32)
                both = jnp.concatenate([dkey, dvalue], axis=1)

                @pl.when(me == kb)
                def _():
                    acc[:, term_cols] = both

                @pl.when(me != kb)
                def _():
                    dsend[at, term_cols] = both.astype(BF16)
                    d_copy(kb, me, term_cols).start()

            return carry

        if nkv == 1:
            one_kv(0, 0)
        else:
            lax.fori_loop(0, nkv, one_kv, 0)

    for group in range(groups):
        pl.when(my_group == group)(functools.partial(work, group))

    everything = pl.ds(0, nkv * 2 * hd)
    for s in range(n_cp):
        @pl.when((me != s) & (my_group <= s // per_group))
        def _():
            d_copy(0, s, everything).wait_recv()
            acc[...] += drecv[s * tokens:(s + 1) * tokens, :].astype(F32)

    for kv in range(nkv):
        kg_ref[0, :, kv * hd:(kv + 1) * hd] = acc[:, kv * 2 * hd:kv * 2 * hd + hd].astype(BF16)
        vg_ref[0, :, kv * hd:(kv + 1) * hd] = acc[:, kv * 2 * hd + hd:(kv + 1) * 2 * hd].astype(BF16)

    for d in range(n_cp):
        @pl.when((me != d) & (my_group <= d // per_group))
        def _():
            for copy in kv_copies(d, me):
                copy.wait_send()

        @pl.when((me != d) & (my_group >= d // per_group))
        def _():
            d_copy(d, me, everything).wait_send()

    @pl.when(sec > 0)
    def _():
        pltpu.make_async_remote_copy(
            src_ref=stag, dst_ref=land, send_sem=dq_send, recv_sem=dq_recv.at[0],
            device_id={"pp": lax.rem(sec + n_pp - 1, n_pp)}, device_id_type=MESH,
        ).wait_send()

    pieces = heads // chunk
    outs = []
    for piece in range(pieces):
        @pl.when(sec < n_pp - 1)
        def _():
            pltpu.make_async_remote_copy(
                src_ref=stag.at[piece], dst_ref=land.at[piece], send_sem=dq_send, recv_sem=dq_recv.at[piece],
                device_id={"pp": lax.rem(sec + n_pp - 1, n_pp)}, device_id_type=MESH,
            ).wait_recv()

        cols = pl.ds(piece * chunk * hd, chunk * hd)
        outs.append(pltpu.make_async_copy(land.at[piece], handed.at[0, :, cols], out_sem.at[piece]))
        outs[-1].start()
    for copy in outs:
        copy.wait()


def finish(handed, kg, vg, handed_out, kg_out, vg_out, handed_buf, kg_buf, vg_buf, sem):
    rows = handed.shape[1] // 4
    trips = [(kg, kg_buf, kg_out), (vg, vg_buf, vg_out)]
    for i in range(4):
        at = (slice(None), pl.ds(i * rows, rows))
        trips.append((handed.at[at], handed_buf.at[at], handed_out.at[at]))
    loads = [pltpu.make_async_copy(a, b, sem.at[0, i]) for i, (a, b, _) in enumerate(trips)]
    stores = [pltpu.make_async_copy(b, c, sem.at[1, i]) for i, (_, b, c) in enumerate(trips)]
    for load in loads:
        load.start()
    for load, store in zip(loads, stores):
        load.wait()
        store.start()
    for store in stores:
        store.wait()


def body(n_pp, n_cp, n_tp, query, key, value, out_grad, lengths, plan):
    tokens, width = query.shape[1], query.shape[2]
    kv_width = key.shape[2]
    hd = 128
    heads, nkv = width // hd, kv_width // hd
    groups = min(n_cp, 4)
    block_rows = tokens // n_cp
    seq = n_cp * tokens
    wide = BF16 if block_rows % 16 == 0 else F32
    chunk = 4
    group_rows = heads // nkv * tokens
    sizes = (n_pp, n_cp, tokens, heads, nkv, hd, lengths.shape[0], groups, chunk)
    hbm = pl.BlockSpec(memory_space=pltpu.HBM)
    vmem = pl.BlockSpec(memory_space=pltpu.VMEM)
    dma = pltpu.SemaphoreType.DMA
    handed, key_grad, value_grad = pl.pallas_call(
        functools.partial(kernel, sizes),
        out_shape=(
            jax.ShapeDtypeStruct(query.shape, wide),
            jax.ShapeDtypeStruct(key.shape, BF16),
            jax.ShapeDtypeStruct(value.shape, BF16),
        ),
        in_specs=[hbm] * 6,
        out_specs=(hbm, vmem, vmem),
        scratch_shapes=[
            pltpu.SMEM(plan.shape, jnp.int32),
            pltpu.SMEM(lengths.shape, jnp.int32),
            pltpu.VMEM((tokens, width), BF16),
            pltpu.VMEM((tokens, width), BF16),
            pltpu.VMEM((heads * tokens, hd), BF16),
            pltpu.VMEM((heads * tokens, hd), BF16),
            pltpu.VMEM((seq, kv_width), BF16),
            pltpu.VMEM((seq, kv_width), BF16),
            pltpu.VMEM((hd, seq), BF16),
            pltpu.VMEM((seq, tokens), F32),
            pltpu.VMEM((seq, group_rows), BF16),
            pltpu.VMEM((seq, group_rows), BF16),
            pltpu.VMEM((heads // chunk, tokens, chunk * hd), wide),
            pltpu.VMEM((heads // chunk, tokens, chunk * hd), wide),
            pltpu.VMEM((tokens, 2 * kv_width), F32),
            pltpu.VMEM((seq, 2 * kv_width), BF16),
            pltpu.VMEM((seq, 2 * kv_width), BF16),
            dma((2,)), dma((2,)), dma((2, n_cp)), dma((2, n_cp)),
            dma, dma((heads // chunk,)), dma((n_cp,)), dma((n_cp,)), dma((heads // chunk,)), dma((2,)),
        ],
        compiler_params=pltpu.CompilerParams(
            collective_id=0, has_side_effects=True, vmem_limit_bytes=VMEM
        ),
        cost_estimate=pl.CostEstimate(
            flops=10 * tokens * heads * seq * hd, bytes_accessed=6 * tokens * width,
            transcendentals=tokens * heads * seq,
        ),
    )(plan, lengths, query, key, value, out_grad)
    if wide != BF16:
        return handed.astype(BF16), key_grad, value_grad
    results = (handed, key_grad, value_grad)
    return pl.pallas_call(
        finish,
        out_shape=tuple(jax.ShapeDtypeStruct(r.shape, r.dtype) for r in results),
        in_specs=[hbm] * 3,
        out_specs=(hbm,) * 3,
        scratch_shapes=[pltpu.VMEM(r.shape, r.dtype) for r in results] + [dma((2, 6))],
        compiler_params=pltpu.CompilerParams(vmem_limit_bytes=VMEM),
    )(*results)


def solution(mesh):
    spec = P("pp", "cp", "tp")
    sizes = (mesh.shape["pp"], mesh.shape["cp"], mesh.shape["tp"])
    return jax.shard_map(
        functools.partial(body, *sizes),
        mesh=mesh,
        in_specs=(spec, spec, spec, spec, P(), P()),
        out_specs=(spec, spec, spec),
        check_vma=False,
    )
```

```python
import functools
import math

import jax
import jax.numpy as jnp
from jax import lax
from jax.experimental import pallas as pl
from jax.experimental.pallas import tpu as pltpu
from jax.sharding import PartitionSpec as P

MESH = pl.DeviceIdType.MESH
F32 = jnp.float32
BF16 = jnp.bfloat16
VMEM = 60 * 2 ** 20
NT = (((1,), (1,)), ((), ()))


def kernel(
    sizes,
    plan_hbm, lens_hbm, q_hbm, k_hbm, v_hbm, g_hbm,
    handed, kg_ref, vg_ref,
    plan_ref, lens_ref, qraw, graw, qs, gs, kall, vall, kt, bias, pst, dst, stag, land, relay, acc, dsend, drecv,
    in_sem, own_sem, kv_send, kv_pass, kv_recv, dq_send, dq_recv, relay_send, relay_recv, d_send, d_recv, out_sem, table_sem,
):
    n_pp, n_cp, tokens, heads, nkv, hd, ndoc, groups, chunk = sizes
    group_heads = heads // nkv
    per_group = n_cp // groups
    block_rows = tokens // n_cp
    me = lax.axis_index("cp")
    sec = lax.axis_index("pp")
    my_group = me // per_group
    scale = hd ** -0.5

    barrier = pltpu.get_barrier_semaphore()

    for d in range(n_cp):
        @pl.when(me != d)
        def _():
            pl.semaphore_signal(barrier, inc=1, device_id={"cp": d}, device_id_type=MESH)

    @pl.when(sec < n_pp - 1)
    def _():
        for d in range(n_cp):
            pl.semaphore_signal(barrier, inc=1, device_id={"pp": sec + 1, "cp": d}, device_id_type=MESH)

    plan_in = pltpu.make_async_copy(plan_hbm, plan_ref, table_sem.at[0])
    lens_in = pltpu.make_async_copy(lens_hbm, lens_ref, table_sem.at[1])
    my_rows = pl.ds(pl.multiple_of(me * tokens, tokens), tokens)
    k_own = pltpu.make_async_copy(k_hbm.at[0], kall.at[my_rows], own_sem.at[0])
    v_own = pltpu.make_async_copy(v_hbm.at[0], vall.at[my_rows], own_sem.at[1])
    q_in = pltpu.make_async_copy(q_hbm.at[0], qraw, in_sem.at[0])
    g_in = pltpu.make_async_copy(g_hbm.at[0], graw, in_sem.at[1])
    for copy in (plan_in, lens_in, k_own, v_own, q_in, g_in):
        copy.start()

    pl.semaphore_wait(barrier, n_cp - 1 + jnp.where(sec > 0, n_cp, 0))

    def kv_copies(d, source, passed):
        rows = pl.ds(pl.multiple_of(source * tokens, tokens), tokens)
        return [
            pltpu.make_async_remote_copy(
                src_ref=full.at[rows] if passed else hbm.at[0], dst_ref=full.at[rows],
                send_sem=kv_pass.at[i, source] if passed else kv_send.at[i, d], recv_sem=kv_recv.at[i, source],
                device_id={"cp": d}, device_id_type=MESH,
            )
            for i, (hbm, full) in enumerate(((k_hbm, kall), (v_hbm, vall)))
        ]

    right = lax.rem(me + 1, n_cp)
    passes = (me % 2 == 0) & (me < n_cp - 1)

    def kv_to(d):
        return me < d if d % 2 == 0 else me == d - 1

    for d in reversed(range(n_cp)):
        @pl.when(kv_to(d))
        def _():
            for copy in kv_copies(d, me, False):
                copy.start()

    @pl.when(sec == n_pp - 1)
    def _():
        land[...] = jnp.zeros_like(land)

    plan_in.wait()
    lens_in.wait()

    def taken_of(slot):
        taken = jnp.zeros_like(slot)
        for d in range(n_cp):
            inverse = jnp.int32(0)
            for j in range(1, n_cp):
                inverse = inverse + jnp.where(plan_ref[me, j] == d, j, 0)
            taken = jnp.where(slot == d, inverse, taken)
        return taken

    row = lax.broadcasted_iota(jnp.int32, (tokens, tokens), 0)
    col = lax.broadcasted_iota(jnp.int32, (tokens, tokens), 1)
    row_slot = row // block_rows
    local = taken_of(row_slot) * block_rows + (row - row_slot * block_rows)
    perm = jnp.where(local == col, 1.0, 0.0).astype(BF16)

    lane = lax.broadcasted_iota(jnp.int32, (1, tokens), 1)
    lane_slot = lane // block_rows
    q_pos = me * tokens + taken_of(lane_slot) * block_rows + (lane - lane_slot * block_rows)
    begin = jnp.zeros_like(q_pos)
    end = jnp.int32(0)
    for i in range(ndoc):
        end = end + lens_ref[i]
        begin = jnp.where(q_pos >= end, end, begin)
    for s in range(n_cp):
        k_pos = lax.broadcasted_iota(jnp.int32, (tokens, tokens), 0) + s * tokens
        seen = (k_pos >= begin) & (k_pos <= q_pos)
        bias[s * tokens:(s + 1) * tokens, :] = jnp.where(seen, 0.0, -jnp.inf)

    q_in.wait()
    g_in.wait()

    def stack(raw, out, c):
        width = 4 * hd
        cols = pl.ds(pl.multiple_of(c * width, width), width)
        moved = jnp.dot(perm, raw[:, cols], preferred_element_type=F32).astype(BF16)
        for h in range(4):
            at = pl.ds(pl.multiple_of((c * 4 + h) * tokens, tokens), tokens)
            out[at, :] = moved[:, h * hd:(h + 1) * hd]

    def stack_both(c, carry):
        stack(qraw, qs, c)
        stack(graw, gs, c)
        return carry

    lax.fori_loop(0, heads // 4, stack_both, 0)
    k_own.wait()
    v_own.wait()

    pieces = heads // chunk
    relayed = pieces // 2
    crosses = (sec > 0) & (sec % 2 == 0)
    forwards = (sec % 2 == 1) & (sec < n_pp - 1)
    before = lax.rem(sec + n_pp - 1, n_pp)
    my_block = pl.ds(pl.multiple_of(me * block_rows, block_rows), block_rows)

    def dq_copy(d, piece):
        return pltpu.make_async_remote_copy(
            src_ref=stag.at[piece, pl.ds(pl.multiple_of(d * block_rows, block_rows), block_rows)],
            dst_ref=land.at[piece, my_block],
            send_sem=dq_send, recv_sem=dq_recv.at[piece],
            device_id={"pp": before, "cp": d}, device_id_type=MESH,
        )

    def cross_copy(off, piece):
        d = lax.rem(me + off, n_cp)
        return pltpu.make_async_remote_copy(
            src_ref=stag.at[piece, pl.ds(pl.multiple_of(d * block_rows, block_rows), block_rows)],
            dst_ref=relay.at[piece, pl.ds((off - 1) * block_rows, block_rows)],
            send_sem=dq_send, recv_sem=relay_recv.at[piece],
            device_id={"pp": before}, device_id_type=MESH,
        )

    def forward(piece):
        pltpu.make_async_remote_copy(
            src_ref=relay.at[piece], dst_ref=relay.at[piece], send_sem=dq_send, recv_sem=relay_recv.at[piece],
            device_id={"pp": before}, device_id_type=MESH,
        ).wait_recv()
        for off in range(1, n_cp):
            pltpu.make_async_remote_copy(
                src_ref=relay.at[piece, pl.ds((off - 1) * block_rows, block_rows)],
                dst_ref=land.at[piece, my_block],
                send_sem=relay_send, recv_sem=dq_recv.at[piece],
                device_id={"cp": lax.rem(me + off, n_cp)}, device_id_type=MESH,
            ).start()

    def send_dq(piece):
        @pl.when(crosses & (piece < relayed))
        def _():
            for off in range(1, n_cp):
                cross_copy(off, piece).start()
            dq_copy(me, piece).start()

        @pl.when((sec > 0) & jnp.logical_not(crosses & (piece < relayed)))
        def _():
            for d in range(n_cp):
                dq_copy(d, piece).start()

        @pl.when(forwards & (piece >= 1) & (piece <= relayed))
        def _():
            forward(piece - 1)

    def d_copy(kb, source, cols):
        at = pl.ds(pl.multiple_of(source * tokens, tokens), tokens)
        return pltpu.make_async_remote_copy(
            src_ref=dsend.at[pl.ds(kb * tokens, tokens), cols],
            dst_ref=drecv.at[at, cols],
            send_sem=d_send.at[kb], recv_sem=d_recv.at[source],
            device_id={"cp": kb}, device_id_type=MESH,
        )

    for s in range(n_cp - 1):
        @pl.when(s < me)
        def _():
            for copy in kv_copies(right, s, True):
                copy.wait_recv()

            @pl.when(passes)
            def _():
                for copy in kv_copies(right, s, True):
                    copy.start()

    def work(group):
        shards = (group + 1) * per_group
        count = shards * tokens
        for s in range(group * per_group + 1, shards):
            @pl.when(me < s)
            def _():
                kall[s * tokens:(s + 1) * tokens, :] = jnp.zeros((tokens, kall.shape[1]), BF16)
                vall[s * tokens:(s + 1) * tokens, :] = jnp.zeros((tokens, vall.shape[1]), BF16)

        def one_kv(kv, carry):
            kv_cols = pl.ds(pl.multiple_of(kv * hd, hd), hd)
            for s in range(shards):
                at = slice(s * tokens, (s + 1) * tokens)
                kt[:, at] = kall[at, kv_cols].astype(F32).T.astype(BF16)

            def one_chunk(c, carry):
                for pair in range(chunk // 2):
                    first = c * chunk + pair * 2
                    rows = pl.ds(pl.multiple_of((kv * group_heads + first) * tokens, 2 * tokens), 2 * tokens)
                    kept = pl.ds(pl.multiple_of(first * tokens, 2 * tokens), 2 * tokens)
                    seen = bias[0:count, :]
                    score = lax.dot_general(kall[0:count, kv_cols], qs[rows, :], NT, preferred_element_type=F32)
                    score = score + jnp.concatenate([seen, seen], axis=1)
                    dprob = lax.dot_general(vall[0:count, kv_cols], gs[rows, :], NT, preferred_element_type=F32)
                    top = jnp.max(score, axis=0, keepdims=True)
                    expo = jnp.exp2((score - top) * (scale * math.log2(math.e)))
                    inverse = 1.0 / jnp.sum(expo, axis=0, keepdims=True)
                    delta = jnp.sum(expo * dprob, axis=0, keepdims=True) * inverse
                    pst[0:count, kept] = (expo * inverse).astype(BF16)
                    dscore = (expo * (inverse * scale) * (dprob - delta)).astype(BF16)
                    dst[0:count, kept] = dscore

                    @pl.when(sec > 0)
                    def _():
                        dqt = jnp.dot(kt[:, 0:count], dscore, preferred_element_type=F32)
                        for h in range(2):
                            at = slice((pair * 2 + h) * hd, (pair * 2 + h + 1) * hd)
                            stag[kv * (group_heads // chunk) + c, :, at] = dqt[:, h * tokens:(h + 1) * tokens].T.astype(stag.dtype)

                send_dq(kv * (group_heads // chunk) + c)
                return carry

            lax.fori_loop(0, group_heads // chunk, one_chunk, 0)

            all_rows = pl.ds(pl.multiple_of(kv * group_heads * tokens, group_heads * tokens), group_heads * tokens)
            term_cols = pl.ds(pl.multiple_of(kv * 2 * hd, 2 * hd), 2 * hd)
            for kb in range(shards):
                at = slice(kb * tokens, (kb + 1) * tokens)
                dkey = jnp.dot(dst[at, :], qs[all_rows, :], preferred_element_type=F32)
                dvalue = jnp.dot(pst[at, :], gs[all_rows, :], preferred_element_type=F32)
                both = jnp.concatenate([dkey, dvalue], axis=1)

                @pl.when(me == kb)
                def _():
                    acc[:, term_cols] = both

                @pl.when(kb < me)
                def _():
                    dsend[at, term_cols] = both.astype(BF16)
                    d_copy(kb, me, term_cols).start()

            return carry

        if nkv == 1:
            one_kv(0, 0)
        else:
            lax.fori_loop(0, nkv, one_kv, 0)

    for group in range(groups):
        pl.when(my_group == group)(functools.partial(work, group))

    everything = pl.ds(0, nkv * 2 * hd)
    for s in range(1, n_cp):
        @pl.when(me < s)
        def _():
            d_copy(0, s, everything).wait_recv()
            acc[...] += drecv[s * tokens:(s + 1) * tokens, :].astype(F32)

    for kv in range(nkv):
        kg_ref[0, :, kv * hd:(kv + 1) * hd] = acc[:, kv * 2 * hd:kv * 2 * hd + hd].astype(BF16)
        vg_ref[0, :, kv * hd:(kv + 1) * hd] = acc[:, kv * 2 * hd + hd:(kv + 1) * 2 * hd].astype(BF16)

    for d in range(n_cp):
        @pl.when(kv_to(d))
        def _():
            for copy in kv_copies(d, me, False):
                copy.wait_send()

        @pl.when((d < me) & passes)
        def _():
            for copy in kv_copies(right, d, True):
                copy.wait_send()

        @pl.when(d < me)
        def _():
            d_copy(d, me, everything).wait_send()

    @pl.when(forwards)
    def _():
        pltpu.make_async_remote_copy(
            src_ref=relay, dst_ref=relay, send_sem=relay_send, recv_sem=relay_recv.at[0],
            device_id={"pp": before}, device_id_type=MESH,
        ).wait_send()

    @pl.when(sec > 0)
    def _():
        pltpu.make_async_remote_copy(
            src_ref=stag, dst_ref=land, send_sem=dq_send, recv_sem=dq_recv.at[0],
            device_id={"pp": lax.rem(sec + n_pp - 1, n_pp)}, device_id_type=MESH,
        ).wait_send()

    outs = []
    for piece in range(pieces):
        @pl.when(sec < n_pp - 1)
        def _():
            pltpu.make_async_remote_copy(
                src_ref=stag.at[piece], dst_ref=land.at[piece], send_sem=dq_send, recv_sem=dq_recv.at[piece],
                device_id={"pp": lax.rem(sec + n_pp - 1, n_pp)}, device_id_type=MESH,
            ).wait_recv()

        cols = pl.ds(piece * chunk * hd, chunk * hd)
        outs.append(pltpu.make_async_copy(land.at[piece], handed.at[0, :, cols], out_sem.at[piece]))
        outs[-1].start()
    for copy in outs:
        copy.wait()


def finish(handed, kg, vg, handed_out, kg_out, vg_out, handed_buf, kg_buf, vg_buf, sem):
    rows = handed.shape[1] // 4
    trips = [(kg, kg_buf, kg_out), (vg, vg_buf, vg_out)]
    for i in range(4):
        at = (slice(None), pl.ds(i * rows, rows))
        trips.append((handed.at[at], handed_buf.at[at], handed_out.at[at]))
    loads = [pltpu.make_async_copy(a, b, sem.at[0, i]) for i, (a, b, _) in enumerate(trips)]
    stores = [pltpu.make_async_copy(b, c, sem.at[1, i]) for i, (_, b, c) in enumerate(trips)]
    for load in loads:
        load.start()
    for load, store in zip(loads, stores):
        load.wait()
        store.start()
    for store in stores:
        store.wait()


def body(n_pp, n_cp, n_tp, query, key, value, out_grad, lengths, plan):
    tokens, width = query.shape[1], query.shape[2]
    kv_width = key.shape[2]
    hd = 128
    heads, nkv = width // hd, kv_width // hd
    groups = min(n_cp, 4)
    block_rows = tokens // n_cp
    seq = n_cp * tokens
    wide = BF16 if block_rows % 16 == 0 else F32
    chunk = 4
    group_rows = heads // nkv * tokens
    sizes = (n_pp, n_cp, tokens, heads, nkv, hd, lengths.shape[0], groups, chunk)
    hbm = pl.BlockSpec(memory_space=pltpu.HBM)
    vmem = pl.BlockSpec(memory_space=pltpu.VMEM)
    dma = pltpu.SemaphoreType.DMA
    handed, key_grad, value_grad = pl.pallas_call(
        functools.partial(kernel, sizes),
        out_shape=(
            jax.ShapeDtypeStruct(query.shape, wide),
            jax.ShapeDtypeStruct(key.shape, BF16),
            jax.ShapeDtypeStruct(value.shape, BF16),
        ),
        in_specs=[hbm] * 6,
        out_specs=(hbm, vmem, vmem),
        scratch_shapes=[
            pltpu.SMEM(plan.shape, jnp.int32),
            pltpu.SMEM(lengths.shape, jnp.int32),
            pltpu.VMEM((tokens, width), BF16),
            pltpu.VMEM((tokens, width), BF16),
            pltpu.VMEM((heads * tokens, hd), BF16),
            pltpu.VMEM((heads * tokens, hd), BF16),
            pltpu.VMEM((seq, kv_width), BF16),
            pltpu.VMEM((seq, kv_width), BF16),
            pltpu.VMEM((hd, seq), BF16),
            pltpu.VMEM((seq, tokens), F32),
            pltpu.VMEM((seq, group_rows), BF16),
            pltpu.VMEM((seq, group_rows), BF16),
            pltpu.VMEM((heads // chunk, tokens, chunk * hd), wide),
            pltpu.VMEM((heads // chunk, tokens, chunk * hd), wide),
            pltpu.VMEM((heads // chunk // 2, tokens - block_rows, chunk * hd), wide),
            pltpu.VMEM((tokens, 2 * kv_width), F32),
            pltpu.VMEM((seq, 2 * kv_width), BF16),
            pltpu.VMEM((seq, 2 * kv_width), BF16),
            dma((2,)), dma((2,)), dma((2, n_cp)), dma((2, n_cp)), dma((2, n_cp)),
            dma, dma((heads // chunk,)), dma, dma((heads // chunk // 2,)), dma((n_cp,)), dma((n_cp,)), dma((heads // chunk,)), dma((2,)),
        ],
        compiler_params=pltpu.CompilerParams(
            collective_id=0, has_side_effects=True, vmem_limit_bytes=VMEM
        ),
        cost_estimate=pl.CostEstimate(
            flops=10 * tokens * heads * seq * hd, bytes_accessed=6 * tokens * width,
            transcendentals=tokens * heads * seq,
        ),
    )(plan, lengths, query, key, value, out_grad)
    if wide != BF16:
        return handed.astype(BF16), key_grad, value_grad
    results = (handed, key_grad, value_grad)
    return pl.pallas_call(
        finish,
        out_shape=tuple(jax.ShapeDtypeStruct(r.shape, r.dtype) for r in results),
        in_specs=[hbm] * 3,
        out_specs=(hbm,) * 3,
        scratch_shapes=[pltpu.VMEM(r.shape, r.dtype) for r in results] + [dma((2, 6))],
        compiler_params=pltpu.CompilerParams(vmem_limit_bytes=VMEM),
    )(*results)


def solution(mesh):
    spec = P("pp", "cp", "tp")
    sizes = (mesh.shape["pp"], mesh.shape["cp"], mesh.shape["tp"])
    return jax.shard_map(
        functools.partial(body, *sizes),
        mesh=mesh,
        in_specs=(spec, spec, spec, spec, P(), P()),
        out_specs=(spec, spec, spec),
        check_vma=False,
    )
```

```python
import functools
import math

import jax
import jax.numpy as jnp
from jax import lax
from jax.experimental import pallas as pl
from jax.experimental.pallas import tpu as pltpu
from jax.sharding import PartitionSpec as P

MESH = pl.DeviceIdType.MESH
F32 = jnp.float32
BF16 = jnp.bfloat16
VMEM = 60 * 2 ** 20
NT = (((1,), (1,)), ((), ()))


def kernel(
    sizes,
    plan_hbm, lens_hbm, q_hbm, k_hbm, v_hbm, g_hbm,
    handed, kg_ref, vg_ref,
    plan_ref, lens_ref, qraw, graw, qs, gs, kall, vall, kt, bias, pst, dst, stag, land, relay, acc, dsend, drecv,
    in_sem, own_sem, kv_send, kv_pass, kv_recv, dq_send, dq_recv, relay_send, relay_recv, d_send, d_recv, out_sem, table_sem,
):
    n_pp, n_cp, tokens, heads, nkv, hd, ndoc, groups, chunk = sizes
    group_heads = heads // nkv
    per_group = n_cp // groups
    block_rows = tokens // n_cp
    me = lax.axis_index("cp")
    sec = lax.axis_index("pp")
    my_group = me // per_group
    scale = hd ** -0.5

    barrier = pltpu.get_barrier_semaphore()

    for d in range(n_cp):
        @pl.when(me != d)
        def _():
            pl.semaphore_signal(barrier, inc=1, device_id={"cp": d}, device_id_type=MESH)

    @pl.when(sec < n_pp - 1)
    def _():
        for d in range(n_cp):
            pl.semaphore_signal(barrier, inc=1, device_id={"pp": sec + 1, "cp": d}, device_id_type=MESH)

    plan_in = pltpu.make_async_copy(plan_hbm, plan_ref, table_sem.at[0])
    lens_in = pltpu.make_async_copy(lens_hbm, lens_ref, table_sem.at[1])
    my_rows = pl.ds(pl.multiple_of(me * tokens, tokens), tokens)
    k_own = pltpu.make_async_copy(k_hbm.at[0], kall.at[my_rows], own_sem.at[0])
    v_own = pltpu.make_async_copy(v_hbm.at[0], vall.at[my_rows], own_sem.at[1])
    q_in = pltpu.make_async_copy(q_hbm.at[0], qraw, in_sem.at[0])
    g_in = pltpu.make_async_copy(g_hbm.at[0], graw, in_sem.at[1])
    for copy in (plan_in, lens_in, k_own, v_own, q_in, g_in):
        copy.start()

    pl.semaphore_wait(barrier, n_cp - 1 + jnp.where(sec > 0, n_cp, 0))

    def kv_copies(d, source, passed):
        rows = pl.ds(pl.multiple_of(source * tokens, tokens), tokens)
        return [
            pltpu.make_async_remote_copy(
                src_ref=full.at[rows] if passed else hbm.at[0], dst_ref=full.at[rows],
                send_sem=kv_pass.at[i, source] if passed else kv_send.at[i, d], recv_sem=kv_recv.at[i, source],
                device_id={"cp": d}, device_id_type=MESH,
            )
            for i, (hbm, full) in enumerate(((k_hbm, kall), (v_hbm, vall)))
        ]

    right = lax.rem(me + 1, n_cp)
    passes = (me % 2 == 0) & (me < n_cp - 1)

    def kv_to(d):
        return me < d if d % 2 == 0 else me == d - 1

    for d in reversed(range(n_cp)):
        @pl.when(kv_to(d))
        def _():
            for copy in kv_copies(d, me, False):
                copy.start()

    @pl.when(sec == n_pp - 1)
    def _():
        land[...] = jnp.zeros_like(land)

    plan_in.wait()
    lens_in.wait()

    def taken_of(slot):
        taken = jnp.zeros_like(slot)
        for d in range(n_cp):
            inverse = jnp.int32(0)
            for j in range(1, n_cp):
                inverse = inverse + jnp.where(plan_ref[me, j] == d, j, 0)
            taken = jnp.where(slot == d, inverse, taken)
        return taken

    row = lax.broadcasted_iota(jnp.int32, (tokens, tokens), 0)
    col = lax.broadcasted_iota(jnp.int32, (tokens, tokens), 1)
    row_slot = row // block_rows
    local = taken_of(row_slot) * block_rows + (row - row_slot * block_rows)
    perm = jnp.where(local == col, 1.0, 0.0).astype(BF16)

    lane = lax.broadcasted_iota(jnp.int32, (1, tokens), 1)
    lane_slot = lane // block_rows
    q_pos = me * tokens + taken_of(lane_slot) * block_rows + (lane - lane_slot * block_rows)
    begin = jnp.zeros_like(q_pos)
    end = jnp.int32(0)
    for i in range(ndoc):
        end = end + lens_ref[i]
        begin = jnp.where(q_pos >= end, end, begin)
    for s in range(n_cp):
        k_pos = lax.broadcasted_iota(jnp.int32, (tokens, tokens), 0) + s * tokens
        seen = (k_pos >= begin) & (k_pos <= q_pos)
        bias[s * tokens:(s + 1) * tokens, :] = jnp.where(seen, 0.0, -jnp.inf)

    q_in.wait()
    g_in.wait()

    def stack(raw, out, c):
        width = 4 * hd
        cols = pl.ds(pl.multiple_of(c * width, width), width)
        moved = jnp.dot(perm, raw[:, cols], preferred_element_type=F32).astype(BF16)
        for h in range(4):
            at = pl.ds(pl.multiple_of((c * 4 + h) * tokens, tokens), tokens)
            out[at, :] = moved[:, h * hd:(h + 1) * hd]

    def stack_both(c, carry):
        stack(qraw, qs, c)
        stack(graw, gs, c)
        return carry

    lax.fori_loop(0, heads // 4, stack_both, 0)
    k_own.wait()
    v_own.wait()

    pieces = heads // chunk
    relayed = pieces // 2
    crosses = (sec > 0) & (sec % 2 == 0)
    forwards = (sec % 2 == 1) & (sec < n_pp - 1)
    before = lax.rem(sec + n_pp - 1, n_pp)
    my_block = pl.ds(pl.multiple_of(me * block_rows, block_rows), block_rows)

    def dq_copy(d, piece):
        return pltpu.make_async_remote_copy(
            src_ref=stag.at[piece, pl.ds(pl.multiple_of(d * block_rows, block_rows), block_rows)],
            dst_ref=land.at[piece, my_block],
            send_sem=dq_send, recv_sem=dq_recv.at[piece],
            device_id={"pp": before, "cp": d}, device_id_type=MESH,
        )

    def cross_copy(off, piece):
        d = lax.rem(me + off, n_cp)
        return pltpu.make_async_remote_copy(
            src_ref=stag.at[piece, pl.ds(pl.multiple_of(d * block_rows, block_rows), block_rows)],
            dst_ref=relay.at[piece, pl.ds((off - 1) * block_rows, block_rows)],
            send_sem=dq_send, recv_sem=relay_recv.at[piece],
            device_id={"pp": before}, device_id_type=MESH,
        )

    def forward(piece):
        pltpu.make_async_remote_copy(
            src_ref=relay.at[piece], dst_ref=relay.at[piece], send_sem=dq_send, recv_sem=relay_recv.at[piece],
            device_id={"pp": before}, device_id_type=MESH,
        ).wait_recv()
        for off in range(1, n_cp):
            pltpu.make_async_remote_copy(
                src_ref=relay.at[piece, pl.ds((off - 1) * block_rows, block_rows)],
                dst_ref=land.at[piece, my_block],
                send_sem=relay_send, recv_sem=dq_recv.at[piece],
                device_id={"cp": lax.rem(me + off, n_cp)}, device_id_type=MESH,
            ).start()

    def send_dq(piece):
        @pl.when(crosses & (piece < relayed))
        def _():
            for off in range(1, n_cp):
                cross_copy(off, piece).start()
            dq_copy(me, piece).start()

        @pl.when((sec > 0) & jnp.logical_not(crosses & (piece < relayed)))
        def _():
            for d in range(n_cp):
                dq_copy(d, piece).start()

    def d_copy(kb, source, cols):
        at = pl.ds(pl.multiple_of(source * tokens, tokens), tokens)
        return pltpu.make_async_remote_copy(
            src_ref=dsend.at[pl.ds(kb * tokens, tokens), cols],
            dst_ref=drecv.at[at, cols],
            send_sem=d_send.at[kb], recv_sem=d_recv.at[source],
            device_id={"cp": kb}, device_id_type=MESH,
        )

    for s in range(n_cp - 1):
        @pl.when(s < me)
        def _():
            for copy in kv_copies(right, s, True):
                copy.wait_recv()

            @pl.when(passes)
            def _():
                for copy in kv_copies(right, s, True):
                    copy.start()

    def work(group):
        shards = (group + 1) * per_group
        count = shards * tokens
        for s in range(group * per_group + 1, shards):
            @pl.when(me < s)
            def _():
                kall[s * tokens:(s + 1) * tokens, :] = jnp.zeros((tokens, kall.shape[1]), BF16)
                vall[s * tokens:(s + 1) * tokens, :] = jnp.zeros((tokens, vall.shape[1]), BF16)

        def one_kv(kv, carry):
            kv_cols = pl.ds(pl.multiple_of(kv * hd, hd), hd)
            for s in range(shards):
                at = slice(s * tokens, (s + 1) * tokens)
                kt[:, at] = kall[at, kv_cols].astype(F32).T.astype(BF16)

            def one_chunk(c, carry):
                for pair in range(chunk // 2):
                    first = c * chunk + pair * 2
                    rows = pl.ds(pl.multiple_of((kv * group_heads + first) * tokens, 2 * tokens), 2 * tokens)
                    kept = pl.ds(pl.multiple_of(first * tokens, 2 * tokens), 2 * tokens)
                    seen = bias[0:count, :]
                    score = lax.dot_general(kall[0:count, kv_cols], qs[rows, :], NT, preferred_element_type=F32)
                    score = score + jnp.concatenate([seen, seen], axis=1)
                    dprob = lax.dot_general(vall[0:count, kv_cols], gs[rows, :], NT, preferred_element_type=F32)
                    top = jnp.max(score, axis=0, keepdims=True)
                    expo = jnp.exp2((score - top) * (scale * math.log2(math.e)))
                    inverse = 1.0 / jnp.sum(expo, axis=0, keepdims=True)
                    delta = jnp.sum(expo * dprob, axis=0, keepdims=True) * inverse
                    pst[0:count, kept] = (expo * inverse).astype(BF16)
                    dscore = (expo * (inverse * scale) * (dprob - delta)).astype(BF16)
                    dst[0:count, kept] = dscore

                    @pl.when(sec > 0)
                    def _():
                        dqt = jnp.dot(kt[:, 0:count], dscore, preferred_element_type=F32)
                        for h in range(2):
                            at = slice((pair * 2 + h) * hd, (pair * 2 + h + 1) * hd)
                            stag[kv * (group_heads // chunk) + c, :, at] = dqt[:, h * tokens:(h + 1) * tokens].T.astype(stag.dtype)

                send_dq(kv * (group_heads // chunk) + c)
                return carry

            lax.fori_loop(0, group_heads // chunk, one_chunk, 0)

            for piece in range(relayed):
                @pl.when(forwards & (kv == piece * chunk * nkv // heads))
                def _():
                    forward(piece)

            all_rows = pl.ds(pl.multiple_of(kv * group_heads * tokens, group_heads * tokens), group_heads * tokens)
            term_cols = pl.ds(pl.multiple_of(kv * 2 * hd, 2 * hd), 2 * hd)
            for kb in range(shards):
                at = slice(kb * tokens, (kb + 1) * tokens)
                dkey = jnp.dot(dst[at, :], qs[all_rows, :], preferred_element_type=F32)
                dvalue = jnp.dot(pst[at, :], gs[all_rows, :], preferred_element_type=F32)
                both = jnp.concatenate([dkey, dvalue], axis=1)

                @pl.when(me == kb)
                def _():
                    acc[:, term_cols] = both

                @pl.when(kb < me)
                def _():
                    dsend[at, term_cols] = both.astype(BF16)
                    d_copy(kb, me, term_cols).start()

            return carry

        if nkv == 1:
            one_kv(0, 0)
        else:
            lax.fori_loop(0, nkv, one_kv, 0)

    for group in range(groups):
        pl.when(my_group == group)(functools.partial(work, group))

    everything = pl.ds(0, nkv * 2 * hd)
    for s in range(1, n_cp):
        @pl.when(me < s)
        def _():
            d_copy(0, s, everything).wait_recv()
            acc[...] += drecv[s * tokens:(s + 1) * tokens, :].astype(F32)

    for kv in range(nkv):
        kg_ref[0, :, kv * hd:(kv + 1) * hd] = acc[:, kv * 2 * hd:kv * 2 * hd + hd].astype(BF16)
        vg_ref[0, :, kv * hd:(kv + 1) * hd] = acc[:, kv * 2 * hd + hd:(kv + 1) * 2 * hd].astype(BF16)

    for d in range(n_cp):
        @pl.when(kv_to(d))
        def _():
            for copy in kv_copies(d, me, False):
                copy.wait_send()

        @pl.when((d < me) & passes)
        def _():
            for copy in kv_copies(right, d, True):
                copy.wait_send()

        @pl.when(d < me)
        def _():
            d_copy(d, me, everything).wait_send()

    @pl.when(forwards)
    def _():
        pltpu.make_async_remote_copy(
            src_ref=relay, dst_ref=relay, send_sem=relay_send, recv_sem=relay_recv.at[0],
            device_id={"pp": before}, device_id_type=MESH,
        ).wait_send()

    @pl.when(sec > 0)
    def _():
        pltpu.make_async_remote_copy(
            src_ref=stag, dst_ref=land, send_sem=dq_send, recv_sem=dq_recv.at[0],
            device_id={"pp": lax.rem(sec + n_pp - 1, n_pp)}, device_id_type=MESH,
        ).wait_send()

    outs = []
    for piece in range(pieces):
        @pl.when(sec < n_pp - 1)
        def _():
            pltpu.make_async_remote_copy(
                src_ref=stag.at[piece], dst_ref=land.at[piece], send_sem=dq_send, recv_sem=dq_recv.at[piece],
                device_id={"pp": lax.rem(sec + n_pp - 1, n_pp)}, device_id_type=MESH,
            ).wait_recv()

        cols = pl.ds(piece * chunk * hd, chunk * hd)
        outs.append(pltpu.make_async_copy(land.at[piece], handed.at[0, :, cols], out_sem.at[piece]))
        outs[-1].start()
    for copy in outs:
        copy.wait()


def finish(handed, kg, vg, handed_out, kg_out, vg_out, handed_buf, kg_buf, vg_buf, sem):
    rows = handed.shape[1] // 4
    trips = [(kg, kg_buf, kg_out), (vg, vg_buf, vg_out)]
    for i in range(4):
        at = (slice(None), pl.ds(i * rows, rows))
        trips.append((handed.at[at], handed_buf.at[at], handed_out.at[at]))
    loads = [pltpu.make_async_copy(a, b, sem.at[0, i]) for i, (a, b, _) in enumerate(trips)]
    stores = [pltpu.make_async_copy(b, c, sem.at[1, i]) for i, (_, b, c) in enumerate(trips)]
    for load in loads:
        load.start()
    for load, store in zip(loads, stores):
        load.wait()
        store.start()
    for store in stores:
        store.wait()


def body(n_pp, n_cp, n_tp, query, key, value, out_grad, lengths, plan):
    tokens, width = query.shape[1], query.shape[2]
    kv_width = key.shape[2]
    hd = 128
    heads, nkv = width // hd, kv_width // hd
    groups = min(n_cp, 4)
    block_rows = tokens // n_cp
    seq = n_cp * tokens
    wide = BF16 if block_rows % 16 == 0 else F32
    chunk = 4
    group_rows = heads // nkv * tokens
    sizes = (n_pp, n_cp, tokens, heads, nkv, hd, lengths.shape[0], groups, chunk)
    hbm = pl.BlockSpec(memory_space=pltpu.HBM)
    vmem = pl.BlockSpec(memory_space=pltpu.VMEM)
    dma = pltpu.SemaphoreType.DMA
    handed, key_grad, value_grad = pl.pallas_call(
        functools.partial(kernel, sizes),
        out_shape=(
            jax.ShapeDtypeStruct(query.shape, wide),
            jax.ShapeDtypeStruct(key.shape, BF16),
            jax.ShapeDtypeStruct(value.shape, BF16),
        ),
        in_specs=[hbm] * 6,
        out_specs=(hbm, vmem, vmem),
        scratch_shapes=[
            pltpu.SMEM(plan.shape, jnp.int32),
            pltpu.SMEM(lengths.shape, jnp.int32),
            pltpu.VMEM((tokens, width), BF16),
            pltpu.VMEM((tokens, width), BF16),
            pltpu.VMEM((heads * tokens, hd), BF16),
            pltpu.VMEM((heads * tokens, hd), BF16),
            pltpu.VMEM((seq, kv_width), BF16),
            pltpu.VMEM((seq, kv_width), BF16),
            pltpu.VMEM((hd, seq), BF16),
            pltpu.VMEM((seq, tokens), F32),
            pltpu.VMEM((seq, group_rows), BF16),
            pltpu.VMEM((seq, group_rows), BF16),
            pltpu.VMEM((heads // chunk, tokens, chunk * hd), wide),
            pltpu.VMEM((heads // chunk, tokens, chunk * hd), wide),
            pltpu.VMEM((heads // chunk // 2, tokens - block_rows, chunk * hd), wide),
            pltpu.VMEM((tokens, 2 * kv_width), F32),
            pltpu.VMEM((seq, 2 * kv_width), BF16),
            pltpu.VMEM((seq, 2 * kv_width), BF16),
            dma((2,)), dma((2,)), dma((2, n_cp)), dma((2, n_cp)), dma((2, n_cp)),
            dma, dma((heads // chunk,)), dma, dma((heads // chunk // 2,)), dma((n_cp,)), dma((n_cp,)), dma((heads // chunk,)), dma((2,)),
        ],
        compiler_params=pltpu.CompilerParams(
            collective_id=0, has_side_effects=True, vmem_limit_bytes=VMEM
        ),
        cost_estimate=pl.CostEstimate(
            flops=10 * tokens * heads * seq * hd, bytes_accessed=6 * tokens * width,
            transcendentals=tokens * heads * seq,
        ),
    )(plan, lengths, query, key, value, out_grad)
    if wide != BF16:
        return handed.astype(BF16), key_grad, value_grad
    results = (handed, key_grad, value_grad)
    return pl.pallas_call(
        finish,
        out_shape=tuple(jax.ShapeDtypeStruct(r.shape, r.dtype) for r in results),
        in_specs=[hbm] * 3,
        out_specs=(hbm,) * 3,
        scratch_shapes=[pltpu.VMEM(r.shape, r.dtype) for r in results] + [dma((2, 6))],
        compiler_params=pltpu.CompilerParams(vmem_limit_bytes=VMEM),
    )(*results)


def solution(mesh):
    spec = P("pp", "cp", "tp")
    sizes = (mesh.shape["pp"], mesh.shape["cp"], mesh.shape["tp"])
    return jax.shard_map(
        functools.partial(body, *sizes),
        mesh=mesh,
        in_specs=(spec, spec, spec, spec, P(), P()),
        out_specs=(spec, spec, spec),
        check_vma=False,
    )
```

```python
import functools
import math

import jax
import jax.numpy as jnp
from jax import lax
from jax.experimental import pallas as pl
from jax.experimental.pallas import tpu as pltpu
from jax.sharding import PartitionSpec as P

MESH = pl.DeviceIdType.MESH
F32 = jnp.float32
BF16 = jnp.bfloat16
VMEM = 60 * 2 ** 20
NT = (((1,), (1,)), ((), ()))


def kernel(
    sizes,
    plan_hbm, lens_hbm, q_hbm, k_hbm, v_hbm, g_hbm,
    handed, kg_ref, vg_ref,
    plan_ref, lens_ref, qraw, graw, qs, gs, kall, vall, kt, bias, pst, dst, stag, land, relay, acc, dsend, drecv,
    in_sem, own_sem, kv_send, kv_recv, dq_send, dq_recv, relay_send, relay_recv, d_send, d_recv, out_sem, table_sem,
):
    n_pp, n_cp, tokens, heads, nkv, hd, ndoc, groups, chunk = sizes
    group_heads = heads // nkv
    per_group = n_cp // groups
    block_rows = tokens // n_cp
    me = lax.axis_index("cp")
    sec = lax.axis_index("pp")
    my_group = me // per_group
    scale = hd ** -0.5

    barrier = pltpu.get_barrier_semaphore()

    for d in range(n_cp):
        @pl.when(me != d)
        def _():
            pl.semaphore_signal(barrier, inc=1, device_id={"cp": d}, device_id_type=MESH)

    @pl.when(sec < n_pp - 1)
    def _():
        for d in range(n_cp):
            pl.semaphore_signal(barrier, inc=1, device_id={"pp": sec + 1, "cp": d}, device_id_type=MESH)

    plan_in = pltpu.make_async_copy(plan_hbm, plan_ref, table_sem.at[0])
    lens_in = pltpu.make_async_copy(lens_hbm, lens_ref, table_sem.at[1])
    my_rows = pl.ds(pl.multiple_of(me * tokens, tokens), tokens)
    k_own = pltpu.make_async_copy(k_hbm.at[0], kall.at[my_rows], own_sem.at[0])
    v_own = pltpu.make_async_copy(v_hbm.at[0], vall.at[my_rows], own_sem.at[1])
    q_in = pltpu.make_async_copy(q_hbm.at[0], qraw, in_sem.at[0])
    g_in = pltpu.make_async_copy(g_hbm.at[0], graw, in_sem.at[1])
    for copy in (plan_in, lens_in, k_own, v_own, q_in, g_in):
        copy.start()

    pl.semaphore_wait(barrier, n_cp - 1 + jnp.where(sec > 0, n_cp, 0))

    def kv_copies(d, source):
        rows = pl.ds(pl.multiple_of(source * tokens, tokens), tokens)
        return [
            pltpu.make_async_remote_copy(
                src_ref=hbm.at[0], dst_ref=full.at[rows],
                send_sem=kv_send.at[i, d], recv_sem=kv_recv.at[i, source],
                device_id={"cp": d}, device_id_type=MESH,
            )
            for i, (hbm, full) in enumerate(((k_hbm, kall), (v_hbm, vall)))
        ]

    for d in reversed(range(1, n_cp)):
        @pl.when(me < d)
        def _():
            for copy in kv_copies(d, me):
                copy.start()

    @pl.when(sec == n_pp - 1)
    def _():
        land[...] = jnp.zeros_like(land)

    plan_in.wait()
    lens_in.wait()

    def taken_of(slot):
        taken = jnp.zeros_like(slot)
        for d in range(n_cp):
            inverse = jnp.int32(0)
            for j in range(1, n_cp):
                inverse = inverse + jnp.where(plan_ref[me, j] == d, j, 0)
            taken = jnp.where(slot == d, inverse, taken)
        return taken

    row = lax.broadcasted_iota(jnp.int32, (tokens, tokens), 0)
    col = lax.broadcasted_iota(jnp.int32, (tokens, tokens), 1)
    row_slot = row // block_rows
    local = taken_of(row_slot) * block_rows + (row - row_slot * block_rows)
    perm = jnp.where(local == col, 1.0, 0.0).astype(BF16)

    lane = lax.broadcasted_iota(jnp.int32, (1, tokens), 1)
    lane_slot = lane // block_rows
    q_pos = me * tokens + taken_of(lane_slot) * block_rows + (lane - lane_slot * block_rows)
    begin = jnp.zeros_like(q_pos)
    end = jnp.int32(0)
    for i in range(ndoc):
        end = end + lens_ref[i]
        begin = jnp.where(q_pos >= end, end, begin)
    for s in range(n_cp):
        k_pos = lax.broadcasted_iota(jnp.int32, (tokens, tokens), 0) + s * tokens
        seen = (k_pos >= begin) & (k_pos <= q_pos)
        bias[s * tokens:(s + 1) * tokens, :] = jnp.where(seen, 0.0, -jnp.inf)

    q_in.wait()
    g_in.wait()

    def stack(raw, out, c):
        width = 4 * hd
        cols = pl.ds(pl.multiple_of(c * width, width), width)
        moved = jnp.dot(perm, raw[:, cols], preferred_element_type=F32).astype(BF16)
        for h in range(4):
            at = pl.ds(pl.multiple_of((c * 4 + h) * tokens, tokens), tokens)
            out[at, :] = moved[:, h * hd:(h + 1) * hd]

    def stack_both(c, carry):
        stack(qraw, qs, c)
        stack(graw, gs, c)
        return carry

    lax.fori_loop(0, heads // 4, stack_both, 0)
    k_own.wait()
    v_own.wait()

    pieces = heads // chunk
    relayed = pieces // 2
    crosses = (sec > 0) & (sec % 2 == 0)
    forwards = (sec % 2 == 1) & (sec < n_pp - 1)
    before = lax.rem(sec + n_pp - 1, n_pp)
    my_block = pl.ds(pl.multiple_of(me * block_rows, block_rows), block_rows)

    def dq_copy(d, piece):
        return pltpu.make_async_remote_copy(
            src_ref=stag.at[piece, pl.ds(pl.multiple_of(d * block_rows, block_rows), block_rows)],
            dst_ref=land.at[piece, my_block],
            send_sem=dq_send, recv_sem=dq_recv.at[piece],
            device_id={"pp": before, "cp": d}, device_id_type=MESH,
        )

    def cross_copy(off, piece):
        d = lax.rem(me + off, n_cp)
        return pltpu.make_async_remote_copy(
            src_ref=stag.at[piece, pl.ds(pl.multiple_of(d * block_rows, block_rows), block_rows)],
            dst_ref=relay.at[piece, pl.ds((off - 1) * block_rows, block_rows)],
            send_sem=dq_send, recv_sem=relay_recv.at[piece],
            device_id={"pp": before}, device_id_type=MESH,
        )

    def forward(piece):
        pltpu.make_async_remote_copy(
            src_ref=relay.at[piece], dst_ref=relay.at[piece], send_sem=dq_send, recv_sem=relay_recv.at[piece],
            device_id={"pp": before}, device_id_type=MESH,
        ).wait_recv()
        for off in range(1, n_cp):
            pltpu.make_async_remote_copy(
                src_ref=relay.at[piece, pl.ds((off - 1) * block_rows, block_rows)],
                dst_ref=land.at[piece, my_block],
                send_sem=relay_send, recv_sem=dq_recv.at[piece],
                device_id={"cp": lax.rem(me + off, n_cp)}, device_id_type=MESH,
            ).start()

    def send_dq(piece):
        @pl.when(crosses & (piece < relayed))
        def _():
            for off in range(1, n_cp):
                cross_copy(off, piece).start()
            dq_copy(me, piece).start()

        @pl.when((sec > 0) & jnp.logical_not(crosses & (piece < relayed)))
        def _():
            for d in range(n_cp):
                dq_copy(d, piece).start()

    def d_copy(kb, source, cols):
        at = pl.ds(pl.multiple_of(source * tokens, tokens), tokens)
        return pltpu.make_async_remote_copy(
            src_ref=dsend.at[pl.ds(kb * tokens, tokens), cols],
            dst_ref=drecv.at[at, cols],
            send_sem=d_send.at[kb], recv_sem=d_recv.at[source],
            device_id={"cp": kb}, device_id_type=MESH,
        )

    for s in range(n_cp - 1):
        @pl.when(s < me)
        def _():
            for copy in kv_copies(n_cp - 1, s):
                copy.wait_recv()

    def work(group):
        shards = (group + 1) * per_group
        count = shards * tokens
        for s in range(group * per_group + 1, shards):
            @pl.when(me < s)
            def _():
                kall[s * tokens:(s + 1) * tokens, :] = jnp.zeros((tokens, kall.shape[1]), BF16)
                vall[s * tokens:(s + 1) * tokens, :] = jnp.zeros((tokens, vall.shape[1]), BF16)

        def one_kv(kv, carry):
            kv_cols = pl.ds(pl.multiple_of(kv * hd, hd), hd)
            for s in range(shards):
                at = slice(s * tokens, (s + 1) * tokens)
                kt[:, at] = kall[at, kv_cols].astype(F32).T.astype(BF16)

            def one_chunk(c, carry):
                for pair in range(chunk // 2):
                    first = c * chunk + pair * 2
                    rows = pl.ds(pl.multiple_of((kv * group_heads + first) * tokens, 2 * tokens), 2 * tokens)
                    kept = pl.ds(pl.multiple_of(first * tokens, 2 * tokens), 2 * tokens)
                    seen = bias[0:count, :]
                    score = lax.dot_general(kall[0:count, kv_cols], qs[rows, :], NT, preferred_element_type=F32)
                    score = score + jnp.concatenate([seen, seen], axis=1)
                    dprob = lax.dot_general(vall[0:count, kv_cols], gs[rows, :], NT, preferred_element_type=F32)
                    top = jnp.max(score, axis=0, keepdims=True)
                    expo = jnp.exp2((score - top) * (scale * math.log2(math.e)))
                    inverse = 1.0 / jnp.sum(expo, axis=0, keepdims=True)
                    delta = jnp.sum(expo * dprob, axis=0, keepdims=True) * inverse
                    pst[0:count, kept] = (expo * inverse).astype(BF16)
                    dscore = (expo * (inverse * scale) * (dprob - delta)).astype(BF16)
                    dst[0:count, kept] = dscore

                    @pl.when(sec > 0)
                    def _():
                        dqt = jnp.dot(kt[:, 0:count], dscore, preferred_element_type=F32)
                        for h in range(2):
                            at = slice((pair * 2 + h) * hd, (pair * 2 + h + 1) * hd)
                            stag[kv * (group_heads // chunk) + c, :, at] = dqt[:, h * tokens:(h + 1) * tokens].T.astype(stag.dtype)

                send_dq(kv * (group_heads // chunk) + c)
                return carry

            lax.fori_loop(0, group_heads // chunk, one_chunk, 0)

            for piece in range(relayed):
                @pl.when(forwards & (kv == piece * chunk * nkv // heads))
                def _():
                    forward(piece)

            all_rows = pl.ds(pl.multiple_of(kv * group_heads * tokens, group_heads * tokens), group_heads * tokens)
            term_cols = pl.ds(pl.multiple_of(kv * 2 * hd, 2 * hd), 2 * hd)
            for kb in range(shards):
                at = slice(kb * tokens, (kb + 1) * tokens)
                dkey = jnp.dot(dst[at, :], qs[all_rows, :], preferred_element_type=F32)
                dvalue = jnp.dot(pst[at, :], gs[all_rows, :], preferred_element_type=F32)
                both = jnp.concatenate([dkey, dvalue], axis=1)

                @pl.when(me == kb)
                def _():
                    acc[:, term_cols] = both

                @pl.when(kb < me)
                def _():
                    dsend[at, term_cols] = both.astype(BF16)
                    d_copy(kb, me, term_cols).start()

            return carry

        if nkv == 1:
            one_kv(0, 0)
        else:
            lax.fori_loop(0, nkv, one_kv, 0)

    for group in range(groups):
        pl.when(my_group == group)(functools.partial(work, group))

    everything = pl.ds(0, nkv * 2 * hd)
    for s in range(1, n_cp):
        @pl.when(me < s)
        def _():
            d_copy(0, s, everything).wait_recv()
            acc[...] += drecv[s * tokens:(s + 1) * tokens, :].astype(F32)

    for kv in range(nkv):
        kg_ref[0, :, kv * hd:(kv + 1) * hd] = acc[:, kv * 2 * hd:kv * 2 * hd + hd].astype(BF16)
        vg_ref[0, :, kv * hd:(kv + 1) * hd] = acc[:, kv * 2 * hd + hd:(kv + 1) * 2 * hd].astype(BF16)

    for d in range(n_cp):
        @pl.when(me < d)
        def _():
            for copy in kv_copies(d, me):
                copy.wait_send()

        @pl.when(d < me)
        def _():
            d_copy(d, me, everything).wait_send()

    @pl.when(forwards)
    def _():
        pltpu.make_async_remote_copy(
            src_ref=relay, dst_ref=relay, send_sem=relay_send, recv_sem=relay_recv.at[0],
            device_id={"pp": before}, device_id_type=MESH,
        ).wait_send()

    @pl.when(sec > 0)
    def _():
        pltpu.make_async_remote_copy(
            src_ref=stag, dst_ref=land, send_sem=dq_send, recv_sem=dq_recv.at[0],
            device_id={"pp": lax.rem(sec + n_pp - 1, n_pp)}, device_id_type=MESH,
        ).wait_send()

    outs = []
    for piece in range(pieces):
        @pl.when(sec < n_pp - 1)
        def _():
            pltpu.make_async_remote_copy(
                src_ref=stag.at[piece], dst_ref=land.at[piece], send_sem=dq_send, recv_sem=dq_recv.at[piece],
                device_id={"pp": lax.rem(sec + n_pp - 1, n_pp)}, device_id_type=MESH,
            ).wait_recv()

        cols = pl.ds(piece * chunk * hd, chunk * hd)
        outs.append(pltpu.make_async_copy(land.at[piece], handed.at[0, :, cols], out_sem.at[piece]))
        outs[-1].start()
    for copy in outs:
        copy.wait()


def finish(handed, kg, vg, handed_out, kg_out, vg_out, handed_buf, kg_buf, vg_buf, sem):
    rows = handed.shape[1] // 4
    trips = [(kg, kg_buf, kg_out), (vg, vg_buf, vg_out)]
    for i in range(4):
        at = (slice(None), pl.ds(i * rows, rows))
        trips.append((handed.at[at], handed_buf.at[at], handed_out.at[at]))
    loads = [pltpu.make_async_copy(a, b, sem.at[0, i]) for i, (a, b, _) in enumerate(trips)]
    stores = [pltpu.make_async_copy(b, c, sem.at[1, i]) for i, (_, b, c) in enumerate(trips)]
    for load in loads:
        load.start()
    for load, store in zip(loads, stores):
        load.wait()
        store.start()
    for store in stores:
        store.wait()


def body(n_pp, n_cp, n_tp, query, key, value, out_grad, lengths, plan):
    tokens, width = query.shape[1], query.shape[2]
    kv_width = key.shape[2]
    hd = 128
    heads, nkv = width // hd, kv_width // hd
    groups = min(n_cp, 4)
    block_rows = tokens // n_cp
    seq = n_cp * tokens
    wide = BF16 if block_rows % 16 == 0 else F32
    chunk = 4
    group_rows = heads // nkv * tokens
    sizes = (n_pp, n_cp, tokens, heads, nkv, hd, lengths.shape[0], groups, chunk)
    hbm = pl.BlockSpec(memory_space=pltpu.HBM)
    vmem = pl.BlockSpec(memory_space=pltpu.VMEM)
    dma = pltpu.SemaphoreType.DMA
    handed, key_grad, value_grad = pl.pallas_call(
        functools.partial(kernel, sizes),
        out_shape=(
            jax.ShapeDtypeStruct(query.shape, wide),
            jax.ShapeDtypeStruct(key.shape, BF16),
            jax.ShapeDtypeStruct(value.shape, BF16),
        ),
        in_specs=[hbm] * 6,
        out_specs=(hbm, vmem, vmem),
        scratch_shapes=[
            pltpu.SMEM(plan.shape, jnp.int32),
            pltpu.SMEM(lengths.shape, jnp.int32),
            pltpu.VMEM((tokens, width), BF16),
            pltpu.VMEM((tokens, width), BF16),
            pltpu.VMEM((heads * tokens, hd), BF16),
            pltpu.VMEM((heads * tokens, hd), BF16),
            pltpu.VMEM((seq, kv_width), BF16),
            pltpu.VMEM((seq, kv_width), BF16),
            pltpu.VMEM((hd, seq), BF16),
            pltpu.VMEM((seq, tokens), F32),
            pltpu.VMEM((seq, group_rows), BF16),
            pltpu.VMEM((seq, group_rows), BF16),
            pltpu.VMEM((heads // chunk, tokens, chunk * hd), wide),
            pltpu.VMEM((heads // chunk, tokens, chunk * hd), wide),
            pltpu.VMEM((heads // chunk // 2, tokens - block_rows, chunk * hd), wide),
            pltpu.VMEM((tokens, 2 * kv_width), F32),
            pltpu.VMEM((seq, 2 * kv_width), BF16),
            pltpu.VMEM((seq, 2 * kv_width), BF16),
            dma((2,)), dma((2,)), dma((2, n_cp)), dma((2, n_cp)),
            dma, dma((heads // chunk,)), dma, dma((heads // chunk // 2,)), dma((n_cp,)), dma((n_cp,)), dma((heads // chunk,)), dma((2,)),
        ],
        compiler_params=pltpu.CompilerParams(
            collective_id=0, has_side_effects=True, vmem_limit_bytes=VMEM
        ),
        cost_estimate=pl.CostEstimate(
            flops=10 * tokens * heads * seq * hd, bytes_accessed=6 * tokens * width,
            transcendentals=tokens * heads * seq,
        ),
    )(plan, lengths, query, key, value, out_grad)
    if wide != BF16:
        return handed.astype(BF16), key_grad, value_grad
    results = (handed, key_grad, value_grad)
    return pl.pallas_call(
        finish,
        out_shape=tuple(jax.ShapeDtypeStruct(r.shape, r.dtype) for r in results),
        in_specs=[hbm] * 3,
        out_specs=(hbm,) * 3,
        scratch_shapes=[pltpu.VMEM(r.shape, r.dtype) for r in results] + [dma((2, 6))],
        compiler_params=pltpu.CompilerParams(vmem_limit_bytes=VMEM),
    )(*results)


def solution(mesh):
    spec = P("pp", "cp", "tp")
    sizes = (mesh.shape["pp"], mesh.shape["cp"], mesh.shape["tp"])
    return jax.shard_map(
        functools.partial(body, *sizes),
        mesh=mesh,
        in_specs=(spec, spec, spec, spec, P(), P()),
        out_specs=(spec, spec, spec),
        check_vma=False,
    )
```

```python
import functools
import math

import jax
import jax.numpy as jnp
from jax import lax
from jax.experimental import pallas as pl
from jax.experimental.pallas import tpu as pltpu
from jax.sharding import PartitionSpec as P

MESH = pl.DeviceIdType.MESH
F32 = jnp.float32
BF16 = jnp.bfloat16
VMEM = 60 * 2 ** 20
NT = (((1,), (1,)), ((), ()))


def kernel(
    sizes,
    plan_hbm, lens_hbm, q_hbm, k_hbm, v_hbm, g_hbm,
    handed, kg_ref, vg_ref,
    plan_ref, lens_ref, qraw, graw, qs, gs, kall, vall, kt, bias, pst, dst, stag, land, relay, acc, dsend, drecv,
    in_sem, own_sem, kv_send, kv_pass, kv_recv, dq_send, dq_recv, relay_send, relay_recv, d_send, d_recv, out_sem, table_sem,
):
    n_pp, n_cp, tokens, heads, nkv, hd, ndoc, groups, chunk = sizes
    group_heads = heads // nkv
    per_group = n_cp // groups
    block_rows = tokens // n_cp
    me = lax.axis_index("cp")
    sec = lax.axis_index("pp")
    my_group = me // per_group
    scale = hd ** -0.5

    barrier = pltpu.get_barrier_semaphore()

    for d in range(n_cp):
        @pl.when(me != d)
        def _():
            pl.semaphore_signal(barrier, inc=1, device_id={"cp": d}, device_id_type=MESH)

    @pl.when(sec < n_pp - 1)
    def _():
        for d in range(n_cp):
            pl.semaphore_signal(barrier, inc=1, device_id={"pp": sec + 1, "cp": d}, device_id_type=MESH)

    plan_in = pltpu.make_async_copy(plan_hbm, plan_ref, table_sem.at[0])
    lens_in = pltpu.make_async_copy(lens_hbm, lens_ref, table_sem.at[1])
    my_rows = pl.ds(pl.multiple_of(me * tokens, tokens), tokens)
    k_own = pltpu.make_async_copy(k_hbm.at[0], kall.at[my_rows], own_sem.at[0])
    v_own = pltpu.make_async_copy(v_hbm.at[0], vall.at[my_rows], own_sem.at[1])
    q_in = pltpu.make_async_copy(q_hbm.at[0], qraw, in_sem.at[0])
    g_in = pltpu.make_async_copy(g_hbm.at[0], graw, in_sem.at[1])
    for copy in (plan_in, lens_in, k_own, v_own, q_in, g_in):
        copy.start()

    pl.semaphore_wait(barrier, n_cp - 1 + jnp.where(sec > 0, n_cp, 0))

    def kv_copies(d, source):
        rows = pl.ds(pl.multiple_of(source * tokens, tokens), tokens)
        return [
            pltpu.make_async_remote_copy(
                src_ref=hbm.at[0], dst_ref=full.at[rows],
                send_sem=kv_send.at[i, d], recv_sem=kv_recv.at[i, source],
                device_id={"cp": d}, device_id_type=MESH,
            )
            for i, (hbm, full) in enumerate(((k_hbm, kall), (v_hbm, vall)))
        ]

    def kv_direct(d):
        return (me < d) & (me != d - 2) if d % 2 else me < d

    for d in reversed(range(1, n_cp)):
        @pl.when(kv_direct(d))
        def _():
            for copy in kv_copies(d, me):
                copy.start()

    odd = me % 2
    passes = (odd == 0) & (me >= 2) & (me < n_cp - 1)
    passed_rows = pl.ds(pl.multiple_of(lax.rem(me + n_cp - 1, n_cp) * tokens, tokens), tokens)
    kv_passed = [
        pltpu.make_async_remote_copy(
            src_ref=full.at[passed_rows], dst_ref=full.at[passed_rows],
            send_sem=kv_pass.at[i], recv_sem=kv_recv.at[i, lax.rem(me + n_cp - 1, n_cp)],
            device_id={"cp": lax.rem(me + 1, n_cp)}, device_id_type=MESH,
        )
        for i, full in enumerate((kall, vall))
    ]

    @pl.when(sec == n_pp - 1)
    def _():
        land[...] = jnp.zeros_like(land)

    plan_in.wait()
    lens_in.wait()

    def taken_of(slot):
        taken = jnp.zeros_like(slot)
        for d in range(n_cp):
            inverse = jnp.int32(0)
            for j in range(1, n_cp):
                inverse = inverse + jnp.where(plan_ref[me, j] == d, j, 0)
            taken = jnp.where(slot == d, inverse, taken)
        return taken

    row = lax.broadcasted_iota(jnp.int32, (tokens, tokens), 0)
    col = lax.broadcasted_iota(jnp.int32, (tokens, tokens), 1)
    row_slot = row // block_rows
    local = taken_of(row_slot) * block_rows + (row - row_slot * block_rows)
    perm = jnp.where(local == col, 1.0, 0.0).astype(BF16)

    lane = lax.broadcasted_iota(jnp.int32, (1, tokens), 1)
    lane_slot = lane // block_rows
    q_pos = me * tokens + taken_of(lane_slot) * block_rows + (lane - lane_slot * block_rows)
    begin = jnp.zeros_like(q_pos)
    end = jnp.int32(0)
    for i in range(ndoc):
        end = end + lens_ref[i]
        begin = jnp.where(q_pos >= end, end, begin)
    for s in range(n_cp):
        k_pos = lax.broadcasted_iota(jnp.int32, (tokens, tokens), 0) + s * tokens
        seen = (k_pos >= begin) & (k_pos <= q_pos)
        bias[s * tokens:(s + 1) * tokens, :] = jnp.where(seen, 0.0, -jnp.inf)

    q_in.wait()
    g_in.wait()

    def stack(raw, out, c):
        width = 4 * hd
        cols = pl.ds(pl.multiple_of(c * width, width), width)
        moved = jnp.dot(perm, raw[:, cols], preferred_element_type=F32).astype(BF16)
        for h in range(4):
            at = pl.ds(pl.multiple_of((c * 4 + h) * tokens, tokens), tokens)
            out[at, :] = moved[:, h * hd:(h + 1) * hd]

    def stack_both(c, carry):
        stack(qraw, qs, c)
        stack(graw, gs, c)
        return carry

    lax.fori_loop(0, heads // 4, stack_both, 0)
    k_own.wait()
    v_own.wait()

    pieces = heads // chunk
    relayed = pieces // 2
    crosses = (sec > 0) & (sec % 2 == 0)
    forwards = (sec % 2 == 1) & (sec < n_pp - 1)
    before = lax.rem(sec + n_pp - 1, n_pp)
    my_block = pl.ds(pl.multiple_of(me * block_rows, block_rows), block_rows)

    def dq_copy(d, piece):
        return pltpu.make_async_remote_copy(
            src_ref=stag.at[piece, pl.ds(pl.multiple_of(d * block_rows, block_rows), block_rows)],
            dst_ref=land.at[piece, my_block],
            send_sem=dq_send, recv_sem=dq_recv.at[piece],
            device_id={"pp": before, "cp": d}, device_id_type=MESH,
        )

    def cross_copy(off, piece):
        d = lax.rem(me + off, n_cp)
        return pltpu.make_async_remote_copy(
            src_ref=stag.at[piece, pl.ds(pl.multiple_of(d * block_rows, block_rows), block_rows)],
            dst_ref=relay.at[piece, pl.ds((off - 1) * block_rows, block_rows)],
            send_sem=dq_send, recv_sem=relay_recv.at[piece],
            device_id={"pp": before}, device_id_type=MESH,
        )

    def forward(piece):
        pltpu.make_async_remote_copy(
            src_ref=relay.at[piece], dst_ref=relay.at[piece], send_sem=dq_send, recv_sem=relay_recv.at[piece],
            device_id={"pp": before}, device_id_type=MESH,
        ).wait_recv()
        for off in range(1, n_cp):
            pltpu.make_async_remote_copy(
                src_ref=relay.at[piece, pl.ds((off - 1) * block_rows, block_rows)],
                dst_ref=land.at[piece, my_block],
                send_sem=relay_send, recv_sem=dq_recv.at[piece],
                device_id={"cp": lax.rem(me + off, n_cp)}, device_id_type=MESH,
            ).start()

    def send_dq(piece):
        @pl.when(crosses & (piece < relayed))
        def _():
            for off in range(1, n_cp):
                cross_copy(off, piece).start()
            dq_copy(me, piece).start()

        @pl.when((sec > 0) & jnp.logical_not(crosses & (piece < relayed)))
        def _():
            for d in range(n_cp):
                dq_copy(d, piece).start()

    def d_copy(kb):
        slot = odd * kb + (1 - odd) * me
        target = odd * (me - 1) + (1 - odd) * kb
        return pltpu.make_async_remote_copy(
            src_ref=dsend.at[pl.ds(kb * tokens, tokens)],
            dst_ref=drecv.at[pl.ds(pl.multiple_of(slot * tokens, tokens), tokens)],
            send_sem=d_send.at[kb], recv_sem=d_recv.at[slot],
            device_id={"cp": target}, device_id_type=MESH,
        )

    def d_arrived(slot):
        at = pl.ds(slot * tokens, tokens)
        pltpu.make_async_remote_copy(
            src_ref=dsend.at[at], dst_ref=drecv.at[at], send_sem=d_send.at[slot], recv_sem=d_recv.at[slot],
            device_id={"cp": lax.rem(me + 1, n_cp)}, device_id_type=MESH,
        ).wait_recv()
        return drecv[slot * tokens:(slot + 1) * tokens, :].astype(F32)

    for s in reversed(range(n_cp - 1)):
        @pl.when(s < me)
        def _():
            for copy in kv_copies(n_cp - 1, s):
                copy.wait_recv()

        @pl.when(passes & (s == me - 1))
        def _():
            for copy in kv_passed:
                copy.start()

    def work(group):
        shards = (group + 1) * per_group
        count = shards * tokens
        for s in range(group * per_group + 1, shards):
            @pl.when(me < s)
            def _():
                kall[s * tokens:(s + 1) * tokens, :] = jnp.zeros((tokens, kall.shape[1]), BF16)
                vall[s * tokens:(s + 1) * tokens, :] = jnp.zeros((tokens, vall.shape[1]), BF16)

        def one_kv(kv, carry):
            kv_cols = pl.ds(pl.multiple_of(kv * hd, hd), hd)
            for s in range(shards):
                at = slice(s * tokens, (s + 1) * tokens)
                kt[:, at] = kall[at, kv_cols].astype(F32).T.astype(BF16)

            def one_chunk(c, carry):
                for pair in range(chunk // 2):
                    first = c * chunk + pair * 2
                    rows = pl.ds(pl.multiple_of((kv * group_heads + first) * tokens, 2 * tokens), 2 * tokens)
                    kept = pl.ds(pl.multiple_of(first * tokens, 2 * tokens), 2 * tokens)
                    seen = bias[0:count, :]
                    score = lax.dot_general(kall[0:count, kv_cols], qs[rows, :], NT, preferred_element_type=F32)
                    score = score + jnp.concatenate([seen, seen], axis=1)
                    dprob = lax.dot_general(vall[0:count, kv_cols], gs[rows, :], NT, preferred_element_type=F32)
                    top = jnp.max(score, axis=0, keepdims=True)
                    expo = jnp.exp2((score - top) * (scale * math.log2(math.e)))
                    inverse = 1.0 / jnp.sum(expo, axis=0, keepdims=True)
                    delta = jnp.sum(expo * dprob, axis=0, keepdims=True) * inverse
                    pst[0:count, kept] = (expo * inverse).astype(BF16)
                    dscore = (expo * (inverse * scale) * (dprob - delta)).astype(BF16)
                    dst[0:count, kept] = dscore

                    @pl.when(sec > 0)
                    def _():
                        dqt = jnp.dot(kt[:, 0:count], dscore, preferred_element_type=F32)
                        for h in range(2):
                            at = slice((pair * 2 + h) * hd, (pair * 2 + h + 1) * hd)
                            stag[kv * (group_heads // chunk) + c, :, at] = dqt[:, h * tokens:(h + 1) * tokens].T.astype(stag.dtype)

                send_dq(kv * (group_heads // chunk) + c)
                return carry

            lax.fori_loop(0, group_heads // chunk, one_chunk, 0)

            for piece in range(relayed):
                @pl.when(forwards & (kv == piece * chunk * nkv // heads))
                def _():
                    forward(piece)

            all_rows = pl.ds(pl.multiple_of(kv * group_heads * tokens, group_heads * tokens), group_heads * tokens)
            term_cols = pl.ds(pl.multiple_of(kv * 2 * hd, 2 * hd), 2 * hd)
            for kb in range(shards):
                at = slice(kb * tokens, (kb + 1) * tokens)
                dkey = jnp.dot(dst[at, :], qs[all_rows, :], preferred_element_type=F32)
                dvalue = jnp.dot(pst[at, :], gs[all_rows, :], preferred_element_type=F32)
                both = jnp.concatenate([dkey, dvalue], axis=1)

                @pl.when(me == kb)
                def _():
                    acc[:, term_cols] = both

                @pl.when(kb < me)
                def _():
                    dsend[at, term_cols] = both.astype(BF16)

                if nkv == 1:
                    @pl.when((kb < me) & (odd == 1))
                    def _():
                        d_copy(kb).start()

            return carry

        if nkv == 1:
            one_kv(0, 0)
        else:
            lax.fori_loop(0, nkv, one_kv, 0)

    for group in range(groups):
        pl.when(my_group == group)(functools.partial(work, group))

    for kb in range(n_cp - 1):
        at = slice(kb * tokens, (kb + 1) * tokens)

        @pl.when((kb < me) & (odd == 0))
        def _():
            dsend[at, :] = (dsend[at, :].astype(F32) + d_arrived(kb)).astype(BF16)
            d_copy(kb).start()

        if nkv > 1:
            @pl.when((kb < me) & (odd == 1))
            def _():
                d_copy(kb).start()

    for e in range(0, n_cp, 2):
        @pl.when(me <= e)
        def _():
            acc[...] += d_arrived(e)

    for kv in range(nkv):
        kg_ref[0, :, kv * hd:(kv + 1) * hd] = acc[:, kv * 2 * hd:kv * 2 * hd + hd].astype(BF16)
        vg_ref[0, :, kv * hd:(kv + 1) * hd] = acc[:, kv * 2 * hd + hd:(kv + 1) * 2 * hd].astype(BF16)

    for d in range(n_cp):
        if d > 0:
            @pl.when(kv_direct(d))
            def _():
                for copy in kv_copies(d, me):
                    copy.wait_send()

        @pl.when(d < me)
        def _():
            d_copy(d).wait_send()

    @pl.when(passes)
    def _():
        for copy in kv_passed:
            copy.wait_send()

    @pl.when(forwards)
    def _():
        pltpu.make_async_remote_copy(
            src_ref=relay, dst_ref=relay, send_sem=relay_send, recv_sem=relay_recv.at[0],
            device_id={"pp": before}, device_id_type=MESH,
        ).wait_send()

    @pl.when(sec > 0)
    def _():
        pltpu.make_async_remote_copy(
            src_ref=stag, dst_ref=land, send_sem=dq_send, recv_sem=dq_recv.at[0],
            device_id={"pp": lax.rem(sec + n_pp - 1, n_pp)}, device_id_type=MESH,
        ).wait_send()

    outs = []
    for piece in range(pieces):
        @pl.when(sec < n_pp - 1)
        def _():
            pltpu.make_async_remote_copy(
                src_ref=stag.at[piece], dst_ref=land.at[piece], send_sem=dq_send, recv_sem=dq_recv.at[piece],
                device_id={"pp": lax.rem(sec + n_pp - 1, n_pp)}, device_id_type=MESH,
            ).wait_recv()

        cols = pl.ds(piece * chunk * hd, chunk * hd)
        outs.append(pltpu.make_async_copy(land.at[piece], handed.at[0, :, cols], out_sem.at[piece]))
        outs[-1].start()
    for copy in outs:
        copy.wait()


def finish(handed, kg, vg, handed_out, kg_out, vg_out, handed_buf, kg_buf, vg_buf, sem):
    rows = handed.shape[1] // 4
    trips = [(kg, kg_buf, kg_out), (vg, vg_buf, vg_out)]
    for i in range(4):
        at = (slice(None), pl.ds(i * rows, rows))
        trips.append((handed.at[at], handed_buf.at[at], handed_out.at[at]))
    loads = [pltpu.make_async_copy(a, b, sem.at[0, i]) for i, (a, b, _) in enumerate(trips)]
    stores = [pltpu.make_async_copy(b, c, sem.at[1, i]) for i, (_, b, c) in enumerate(trips)]
    for load in loads:
        load.start()
    for load, store in zip(loads, stores):
        load.wait()
        store.start()
    for store in stores:
        store.wait()


def body(n_pp, n_cp, n_tp, query, key, value, out_grad, lengths, plan):
    tokens, width = query.shape[1], query.shape[2]
    kv_width = key.shape[2]
    hd = 128
    heads, nkv = width // hd, kv_width // hd
    groups = min(n_cp, 4)
    block_rows = tokens // n_cp
    seq = n_cp * tokens
    wide = BF16 if block_rows % 16 == 0 else F32
    chunk = 4
    group_rows = heads // nkv * tokens
    sizes = (n_pp, n_cp, tokens, heads, nkv, hd, lengths.shape[0], groups, chunk)
    hbm = pl.BlockSpec(memory_space=pltpu.HBM)
    vmem = pl.BlockSpec(memory_space=pltpu.VMEM)
    dma = pltpu.SemaphoreType.DMA
    handed, key_grad, value_grad = pl.pallas_call(
        functools.partial(kernel, sizes),
        out_shape=(
            jax.ShapeDtypeStruct(query.shape, wide),
            jax.ShapeDtypeStruct(key.shape, BF16),
            jax.ShapeDtypeStruct(value.shape, BF16),
        ),
        in_specs=[hbm] * 6,
        out_specs=(hbm, vmem, vmem),
        scratch_shapes=[
            pltpu.SMEM(plan.shape, jnp.int32),
            pltpu.SMEM(lengths.shape, jnp.int32),
            pltpu.VMEM((tokens, width), BF16),
            pltpu.VMEM((tokens, width), BF16),
            pltpu.VMEM((heads * tokens, hd), BF16),
            pltpu.VMEM((heads * tokens, hd), BF16),
            pltpu.VMEM((seq, kv_width), BF16),
            pltpu.VMEM((seq, kv_width), BF16),
            pltpu.VMEM((hd, seq), BF16),
            pltpu.VMEM((seq, tokens), F32),
            pltpu.VMEM((seq, group_rows), BF16),
            pltpu.VMEM((seq, group_rows), BF16),
            pltpu.VMEM((heads // chunk, tokens, chunk * hd), wide),
            pltpu.VMEM((heads // chunk, tokens, chunk * hd), wide),
            pltpu.VMEM((heads // chunk // 2, tokens - block_rows, chunk * hd), wide),
            pltpu.VMEM((tokens, 2 * kv_width), F32),
            pltpu.VMEM((seq, 2 * kv_width), BF16),
            pltpu.VMEM((seq, 2 * kv_width), BF16),
            dma((2,)), dma((2,)), dma((2, n_cp)), dma((2,)), dma((2, n_cp)),
            dma, dma((heads // chunk,)), dma, dma((heads // chunk // 2,)), dma((n_cp,)), dma((n_cp,)), dma((heads // chunk,)), dma((2,)),
        ],
        compiler_params=pltpu.CompilerParams(
            collective_id=0, has_side_effects=True, vmem_limit_bytes=VMEM
        ),
        cost_estimate=pl.CostEstimate(
            flops=10 * tokens * heads * seq * hd, bytes_accessed=6 * tokens * width,
            transcendentals=tokens * heads * seq,
        ),
    )(plan, lengths, query, key, value, out_grad)
    if wide != BF16:
        return handed.astype(BF16), key_grad, value_grad
    results = (handed, key_grad, value_grad)
    return pl.pallas_call(
        finish,
        out_shape=tuple(jax.ShapeDtypeStruct(r.shape, r.dtype) for r in results),
        in_specs=[hbm] * 3,
        out_specs=(hbm,) * 3,
        scratch_shapes=[pltpu.VMEM(r.shape, r.dtype) for r in results] + [dma((2, 6))],
        compiler_params=pltpu.CompilerParams(vmem_limit_bytes=VMEM),
    )(*results)


def solution(mesh):
    spec = P("pp", "cp", "tp")
    sizes = (mesh.shape["pp"], mesh.shape["cp"], mesh.shape["tp"])
    return jax.shard_map(
        functools.partial(body, *sizes),
        mesh=mesh,
        in_specs=(spec, spec, spec, spec, P(), P()),
        out_specs=(spec, spec, spec),
        check_vma=False,
    )
```

```python
import functools
import math

import jax
import jax.numpy as jnp
from jax import lax
from jax.experimental import pallas as pl
from jax.experimental.pallas import tpu as pltpu
from jax.sharding import PartitionSpec as P

MESH = pl.DeviceIdType.MESH
F32 = jnp.float32
BF16 = jnp.bfloat16
VMEM = 60 * 2 ** 20
NT = (((1,), (1,)), ((), ()))


def kernel(
    sizes,
    plan_hbm, lens_hbm, q_hbm, k_hbm, v_hbm, g_hbm,
    handed, kg_ref, vg_ref,
    plan_ref, lens_ref, qraw, graw, qs, gs, kall, vall, kt, bias, pst, dst, stag, land, relay, acc, dsend, drecv,
    in_sem, own_sem, kv_send, kv_recv, dq_send, dq_recv, relay_send, relay_recv, d_send, d_recv, out_sem, table_sem,
):
    n_pp, n_cp, tokens, heads, nkv, hd, ndoc, groups, chunk = sizes
    group_heads = heads // nkv
    per_group = n_cp // groups
    block_rows = tokens // n_cp
    me = lax.axis_index("cp")
    sec = lax.axis_index("pp")
    my_group = me // per_group
    scale = hd ** -0.5

    barrier = pltpu.get_barrier_semaphore()

    for d in range(n_cp):
        @pl.when(me != d)
        def _():
            pl.semaphore_signal(barrier, inc=1, device_id={"cp": d}, device_id_type=MESH)

    @pl.when(sec < n_pp - 1)
    def _():
        for d in range(n_cp):
            pl.semaphore_signal(barrier, inc=1, device_id={"pp": sec + 1, "cp": d}, device_id_type=MESH)

    plan_in = pltpu.make_async_copy(plan_hbm, plan_ref, table_sem.at[0])
    lens_in = pltpu.make_async_copy(lens_hbm, lens_ref, table_sem.at[1])
    my_rows = pl.ds(pl.multiple_of(me * tokens, tokens), tokens)
    k_own = pltpu.make_async_copy(k_hbm.at[0], kall.at[my_rows], own_sem.at[0])
    v_own = pltpu.make_async_copy(v_hbm.at[0], vall.at[my_rows], own_sem.at[1])
    q_in = pltpu.make_async_copy(q_hbm.at[0], qraw, in_sem.at[0])
    g_in = pltpu.make_async_copy(g_hbm.at[0], graw, in_sem.at[1])
    for copy in (plan_in, lens_in, k_own, v_own, q_in, g_in):
        copy.start()

    pl.semaphore_wait(barrier, n_cp - 1 + jnp.where(sec > 0, n_cp, 0))

    def kv_copies(d, source):
        rows = pl.ds(pl.multiple_of(source * tokens, tokens), tokens)
        return [
            pltpu.make_async_remote_copy(
                src_ref=hbm.at[0], dst_ref=full.at[rows],
                send_sem=kv_send.at[i, d], recv_sem=kv_recv.at[i, source],
                device_id={"cp": d}, device_id_type=MESH,
            )
            for i, (hbm, full) in enumerate(((k_hbm, kall), (v_hbm, vall)))
        ]

    for d in reversed(range(1, n_cp)):
        @pl.when(me < d)
        def _():
            for copy in kv_copies(d, me):
                copy.start()

    odd = me % 2

    @pl.when(sec == n_pp - 1)
    def _():
        land[...] = jnp.zeros_like(land)

    plan_in.wait()
    lens_in.wait()

    def taken_of(slot):
        taken = jnp.zeros_like(slot)
        for d in range(n_cp):
            inverse = jnp.int32(0)
            for j in range(1, n_cp):
                inverse = inverse + jnp.where(plan_ref[me, j] == d, j, 0)
            taken = jnp.where(slot == d, inverse, taken)
        return taken

    row = lax.broadcasted_iota(jnp.int32, (tokens, tokens), 0)
    col = lax.broadcasted_iota(jnp.int32, (tokens, tokens), 1)
    row_slot = row // block_rows
    local = taken_of(row_slot) * block_rows + (row - row_slot * block_rows)
    perm = jnp.where(local == col, 1.0, 0.0).astype(BF16)

    lane = lax.broadcasted_iota(jnp.int32, (1, tokens), 1)
    lane_slot = lane // block_rows
    q_pos = me * tokens + taken_of(lane_slot) * block_rows + (lane - lane_slot * block_rows)
    begin = jnp.zeros_like(q_pos)
    end = jnp.int32(0)
    for i in range(ndoc):
        end = end + lens_ref[i]
        begin = jnp.where(q_pos >= end, end, begin)
    for s in range(n_cp):
        k_pos = lax.broadcasted_iota(jnp.int32, (tokens, tokens), 0) + s * tokens
        seen = (k_pos >= begin) & (k_pos <= q_pos)
        bias[s * tokens:(s + 1) * tokens, :] = jnp.where(seen, 0.0, -jnp.inf)

    q_in.wait()
    g_in.wait()

    def stack(raw, out, c):
        width = 4 * hd
        cols = pl.ds(pl.multiple_of(c * width, width), width)
        moved = jnp.dot(perm, raw[:, cols], preferred_element_type=F32).astype(BF16)
        for h in range(4):
            at = pl.ds(pl.multiple_of((c * 4 + h) * tokens, tokens), tokens)
            out[at, :] = moved[:, h * hd:(h + 1) * hd]

    def stack_both(c, carry):
        stack(qraw, qs, c)
        stack(graw, gs, c)
        return carry

    lax.fori_loop(0, heads // 4, stack_both, 0)
    k_own.wait()
    v_own.wait()

    pieces = heads // chunk
    relayed = pieces // 2
    crosses = (sec > 0) & (sec % 2 == 0)
    forwards = (sec % 2 == 1) & (sec < n_pp - 1)
    before = lax.rem(sec + n_pp - 1, n_pp)
    my_block = pl.ds(pl.multiple_of(me * block_rows, block_rows), block_rows)

    def dq_copy(d, piece):
        return pltpu.make_async_remote_copy(
            src_ref=stag.at[piece, pl.ds(pl.multiple_of(d * block_rows, block_rows), block_rows)],
            dst_ref=land.at[piece, my_block],
            send_sem=dq_send, recv_sem=dq_recv.at[piece],
            device_id={"pp": before, "cp": d}, device_id_type=MESH,
        )

    def cross_copy(off, piece):
        d = lax.rem(me + off, n_cp)
        return pltpu.make_async_remote_copy(
            src_ref=stag.at[piece, pl.ds(pl.multiple_of(d * block_rows, block_rows), block_rows)],
            dst_ref=relay.at[piece, pl.ds((off - 1) * block_rows, block_rows)],
            send_sem=dq_send, recv_sem=relay_recv.at[piece],
            device_id={"pp": before}, device_id_type=MESH,
        )

    def forward(piece):
        pltpu.make_async_remote_copy(
            src_ref=relay.at[piece], dst_ref=relay.at[piece], send_sem=dq_send, recv_sem=relay_recv.at[piece],
            device_id={"pp": before}, device_id_type=MESH,
        ).wait_recv()
        for off in range(1, n_cp):
            pltpu.make_async_remote_copy(
                src_ref=relay.at[piece, pl.ds((off - 1) * block_rows, block_rows)],
                dst_ref=land.at[piece, my_block],
                send_sem=relay_send, recv_sem=dq_recv.at[piece],
                device_id={"cp": lax.rem(me + off, n_cp)}, device_id_type=MESH,
            ).start()

    def send_dq(piece):
        @pl.when(crosses & (piece < relayed))
        def _():
            for off in range(1, n_cp):
                cross_copy(off, piece).start()
            dq_copy(me, piece).start()

        @pl.when((sec > 0) & jnp.logical_not(crosses & (piece < relayed)))
        def _():
            for d in range(n_cp):
                dq_copy(d, piece).start()

    def d_copy(kb):
        slot = odd * kb + (1 - odd) * me
        target = odd * (me - 1) + (1 - odd) * kb
        return pltpu.make_async_remote_copy(
            src_ref=dsend.at[pl.ds(kb * tokens, tokens)],
            dst_ref=drecv.at[pl.ds(pl.multiple_of(slot * tokens, tokens), tokens)],
            send_sem=d_send.at[kb], recv_sem=d_recv.at[slot],
            device_id={"cp": target}, device_id_type=MESH,
        )

    def d_arrived(slot):
        at = pl.ds(slot * tokens, tokens)
        pltpu.make_async_remote_copy(
            src_ref=dsend.at[at], dst_ref=drecv.at[at], send_sem=d_send.at[slot], recv_sem=d_recv.at[slot],
            device_id={"cp": lax.rem(me + 1, n_cp)}, device_id_type=MESH,
        ).wait_recv()
        return drecv[slot * tokens:(slot + 1) * tokens, :].astype(F32)

    for s in range(n_cp - 1):
        @pl.when(s < me)
        def _():
            for copy in kv_copies(n_cp - 1, s):
                copy.wait_recv()

    def work(group):
        shards = (group + 1) * per_group
        count = shards * tokens
        for s in range(group * per_group + 1, shards):
            @pl.when(me < s)
            def _():
                kall[s * tokens:(s + 1) * tokens, :] = jnp.zeros((tokens, kall.shape[1]), BF16)
                vall[s * tokens:(s + 1) * tokens, :] = jnp.zeros((tokens, vall.shape[1]), BF16)

        def one_kv(kv, carry):
            kv_cols = pl.ds(pl.multiple_of(kv * hd, hd), hd)
            for s in range(shards):
                at = slice(s * tokens, (s + 1) * tokens)
                kt[:, at] = kall[at, kv_cols].astype(F32).T.astype(BF16)

            def one_chunk(c, carry):
                for pair in range(chunk // 2):
                    first = c * chunk + pair * 2
                    rows = pl.ds(pl.multiple_of((kv * group_heads + first) * tokens, 2 * tokens), 2 * tokens)
                    kept = pl.ds(pl.multiple_of(first * tokens, 2 * tokens), 2 * tokens)
                    seen = bias[0:count, :]
                    score = lax.dot_general(kall[0:count, kv_cols], qs[rows, :], NT, preferred_element_type=F32)
                    score = score + jnp.concatenate([seen, seen], axis=1)
                    dprob = lax.dot_general(vall[0:count, kv_cols], gs[rows, :], NT, preferred_element_type=F32)
                    top = jnp.max(score, axis=0, keepdims=True)
                    expo = jnp.exp2((score - top) * (scale * math.log2(math.e)))
                    inverse = 1.0 / jnp.sum(expo, axis=0, keepdims=True)
                    delta = jnp.sum(expo * dprob, axis=0, keepdims=True) * inverse
                    pst[0:count, kept] = (expo * inverse).astype(BF16)
                    dscore = (expo * (inverse * scale) * (dprob - delta)).astype(BF16)
                    dst[0:count, kept] = dscore

                    @pl.when(sec > 0)
                    def _():
                        dqt = jnp.dot(kt[:, 0:count], dscore, preferred_element_type=F32)
                        for h in range(2):
                            at = slice((pair * 2 + h) * hd, (pair * 2 + h + 1) * hd)
                            stag[kv * (group_heads // chunk) + c, :, at] = dqt[:, h * tokens:(h + 1) * tokens].T.astype(stag.dtype)

                send_dq(kv * (group_heads // chunk) + c)
                return carry

            lax.fori_loop(0, group_heads // chunk, one_chunk, 0)

            for piece in range(relayed):
                @pl.when(forwards & (kv == piece * chunk * nkv // heads))
                def _():
                    forward(piece)

            all_rows = pl.ds(pl.multiple_of(kv * group_heads * tokens, group_heads * tokens), group_heads * tokens)
            term_cols = pl.ds(pl.multiple_of(kv * 2 * hd, 2 * hd), 2 * hd)
            for kb in range(shards):
                at = slice(kb * tokens, (kb + 1) * tokens)
                dkey = jnp.dot(dst[at, :], qs[all_rows, :], preferred_element_type=F32)
                dvalue = jnp.dot(pst[at, :], gs[all_rows, :], preferred_element_type=F32)
                both = jnp.concatenate([dkey, dvalue], axis=1)

                @pl.when(me == kb)
                def _():
                    acc[:, term_cols] = both

                @pl.when(kb < me)
                def _():
                    dsend[at, term_cols] = both.astype(BF16)

                if nkv == 1:
                    @pl.when((kb < me) & (odd == 1))
                    def _():
                        d_copy(kb).start()

            return carry

        if nkv == 1:
            one_kv(0, 0)
        else:
            lax.fori_loop(0, nkv, one_kv, 0)

    for group in range(groups):
        pl.when(my_group == group)(functools.partial(work, group))

    for kb in range(n_cp - 1):
        at = slice(kb * tokens, (kb + 1) * tokens)

        @pl.when((kb < me) & (odd == 0))
        def _():
            dsend[at, :] = (dsend[at, :].astype(F32) + d_arrived(kb)).astype(BF16)
            d_copy(kb).start()

        if nkv > 1:
            @pl.when((kb < me) & (odd == 1))
            def _():
                d_copy(kb).start()

    for e in range(0, n_cp, 2):
        @pl.when(me <= e)
        def _():
            acc[...] += d_arrived(e)

    for kv in range(nkv):
        kg_ref[0, :, kv * hd:(kv + 1) * hd] = acc[:, kv * 2 * hd:kv * 2 * hd + hd].astype(BF16)
        vg_ref[0, :, kv * hd:(kv + 1) * hd] = acc[:, kv * 2 * hd + hd:(kv + 1) * 2 * hd].astype(BF16)

    for d in range(n_cp):
        @pl.when(me < d)
        def _():
            for copy in kv_copies(d, me):
                copy.wait_send()

        @pl.when(d < me)
        def _():
            d_copy(d).wait_send()

    @pl.when(forwards)
    def _():
        pltpu.make_async_remote_copy(
            src_ref=relay, dst_ref=relay, send_sem=relay_send, recv_sem=relay_recv.at[0],
            device_id={"pp": before}, device_id_type=MESH,
        ).wait_send()

    @pl.when(sec > 0)
    def _():
        pltpu.make_async_remote_copy(
            src_ref=stag, dst_ref=land, send_sem=dq_send, recv_sem=dq_recv.at[0],
            device_id={"pp": lax.rem(sec + n_pp - 1, n_pp)}, device_id_type=MESH,
        ).wait_send()

    outs = []
    for piece in range(pieces):
        @pl.when(sec < n_pp - 1)
        def _():
            pltpu.make_async_remote_copy(
                src_ref=stag.at[piece], dst_ref=land.at[piece], send_sem=dq_send, recv_sem=dq_recv.at[piece],
                device_id={"pp": lax.rem(sec + n_pp - 1, n_pp)}, device_id_type=MESH,
            ).wait_recv()

        cols = pl.ds(piece * chunk * hd, chunk * hd)
        outs.append(pltpu.make_async_copy(land.at[piece], handed.at[0, :, cols], out_sem.at[piece]))
        outs[-1].start()
    for copy in outs:
        copy.wait()


def finish(handed, kg, vg, handed_out, kg_out, vg_out, handed_buf, kg_buf, vg_buf, sem):
    rows = handed.shape[1] // 4
    trips = [(kg, kg_buf, kg_out), (vg, vg_buf, vg_out)]
    for i in range(4):
        at = (slice(None), pl.ds(i * rows, rows))
        trips.append((handed.at[at], handed_buf.at[at], handed_out.at[at]))
    loads = [pltpu.make_async_copy(a, b, sem.at[0, i]) for i, (a, b, _) in enumerate(trips)]
    stores = [pltpu.make_async_copy(b, c, sem.at[1, i]) for i, (_, b, c) in enumerate(trips)]
    for load in loads:
        load.start()
    for load, store in zip(loads, stores):
        load.wait()
        store.start()
    for store in stores:
        store.wait()


def body(n_pp, n_cp, n_tp, query, key, value, out_grad, lengths, plan):
    tokens, width = query.shape[1], query.shape[2]
    kv_width = key.shape[2]
    hd = 128
    heads, nkv = width // hd, kv_width // hd
    groups = min(n_cp, 4)
    block_rows = tokens // n_cp
    seq = n_cp * tokens
    wide = BF16 if block_rows % 16 == 0 else F32
    chunk = 4
    group_rows = heads // nkv * tokens
    sizes = (n_pp, n_cp, tokens, heads, nkv, hd, lengths.shape[0], groups, chunk)
    hbm = pl.BlockSpec(memory_space=pltpu.HBM)
    vmem = pl.BlockSpec(memory_space=pltpu.VMEM)
    dma = pltpu.SemaphoreType.DMA
    handed, key_grad, value_grad = pl.pallas_call(
        functools.partial(kernel, sizes),
        out_shape=(
            jax.ShapeDtypeStruct(query.shape, wide),
            jax.ShapeDtypeStruct(key.shape, BF16),
            jax.ShapeDtypeStruct(value.shape, BF16),
        ),
        in_specs=[hbm] * 6,
        out_specs=(hbm, vmem, vmem),
        scratch_shapes=[
            pltpu.SMEM(plan.shape, jnp.int32),
            pltpu.SMEM(lengths.shape, jnp.int32),
            pltpu.VMEM((tokens, width), BF16),
            pltpu.VMEM((tokens, width), BF16),
            pltpu.VMEM((heads * tokens, hd), BF16),
            pltpu.VMEM((heads * tokens, hd), BF16),
            pltpu.VMEM((seq, kv_width), BF16),
            pltpu.VMEM((seq, kv_width), BF16),
            pltpu.VMEM((hd, seq), BF16),
            pltpu.VMEM((seq, tokens), F32),
            pltpu.VMEM((seq, group_rows), BF16),
            pltpu.VMEM((seq, group_rows), BF16),
            pltpu.VMEM((heads // chunk, tokens, chunk * hd), wide),
            pltpu.VMEM((heads // chunk, tokens, chunk * hd), wide),
            pltpu.VMEM((heads // chunk // 2, tokens - block_rows, chunk * hd), wide),
            pltpu.VMEM((tokens, 2 * kv_width), F32),
            pltpu.VMEM((seq, 2 * kv_width), BF16),
            pltpu.VMEM((seq, 2 * kv_width), BF16),
            dma((2,)), dma((2,)), dma((2, n_cp)), dma((2, n_cp)),
            dma, dma((heads // chunk,)), dma, dma((heads // chunk // 2,)), dma((n_cp,)), dma((n_cp,)), dma((heads // chunk,)), dma((2,)),
        ],
        compiler_params=pltpu.CompilerParams(
            collective_id=0, has_side_effects=True, vmem_limit_bytes=VMEM
        ),
        cost_estimate=pl.CostEstimate(
            flops=10 * tokens * heads * seq * hd, bytes_accessed=6 * tokens * width,
            transcendentals=tokens * heads * seq,
        ),
    )(plan, lengths, query, key, value, out_grad)
    if wide != BF16:
        return handed.astype(BF16), key_grad, value_grad
    results = (handed, key_grad, value_grad)
    return pl.pallas_call(
        finish,
        out_shape=tuple(jax.ShapeDtypeStruct(r.shape, r.dtype) for r in results),
        in_specs=[hbm] * 3,
        out_specs=(hbm,) * 3,
        scratch_shapes=[pltpu.VMEM(r.shape, r.dtype) for r in results] + [dma((2, 6))],
        compiler_params=pltpu.CompilerParams(vmem_limit_bytes=VMEM),
    )(*results)


def solution(mesh):
    spec = P("pp", "cp", "tp")
    sizes = (mesh.shape["pp"], mesh.shape["cp"], mesh.shape["tp"])
    return jax.shard_map(
        functools.partial(body, *sizes),
        mesh=mesh,
        in_specs=(spec, spec, spec, spec, P(), P()),
        out_specs=(spec, spec, spec),
        check_vma=False,
    )
```

```python
import functools
import math

import jax
import jax.numpy as jnp
from jax import lax
from jax.experimental import pallas as pl
from jax.experimental.pallas import tpu as pltpu
from jax.sharding import PartitionSpec as P

MESH = pl.DeviceIdType.MESH
F32 = jnp.float32
BF16 = jnp.bfloat16
VMEM = 60 * 2 ** 20
NT = (((1,), (1,)), ((), ()))


def kernel(
    sizes,
    plan_hbm, lens_hbm, q_hbm, k_hbm, v_hbm, g_hbm,
    handed, kg_ref, vg_ref,
    plan_ref, lens_ref, qraw, graw, qs, gs, kall, vall, kt, bias, pst, dst, stag, land, relay, acc, dsend, drecv,
    in_sem, own_sem, kv_send, kv_recv, dq_send, dq_recv, relay_send, relay_recv, d_send, d_recv, out_sem, table_sem,
):
    n_pp, n_cp, tokens, heads, nkv, hd, ndoc, groups, chunk = sizes
    group_heads = heads // nkv
    per_group = n_cp // groups
    block_rows = tokens // n_cp
    me = lax.axis_index("cp")
    sec = lax.axis_index("pp")
    my_group = me // per_group
    scale = hd ** -0.5

    barrier = pltpu.get_barrier_semaphore()

    for d in range(n_cp):
        @pl.when(me != d)
        def _():
            pl.semaphore_signal(barrier, inc=1, device_id={"cp": d}, device_id_type=MESH)

    @pl.when(sec < n_pp - 1)
    def _():
        for d in range(n_cp):
            pl.semaphore_signal(barrier, inc=1, device_id={"pp": sec + 1, "cp": d}, device_id_type=MESH)

    plan_in = pltpu.make_async_copy(plan_hbm, plan_ref, table_sem.at[0])
    lens_in = pltpu.make_async_copy(lens_hbm, lens_ref, table_sem.at[1])
    my_rows = pl.ds(pl.multiple_of(me * tokens, tokens), tokens)
    k_own = pltpu.make_async_copy(k_hbm.at[0], kall.at[my_rows], own_sem.at[0])
    v_own = pltpu.make_async_copy(v_hbm.at[0], vall.at[my_rows], own_sem.at[1])
    q_in = pltpu.make_async_copy(q_hbm.at[0], qraw, in_sem.at[0])
    g_in = pltpu.make_async_copy(g_hbm.at[0], graw, in_sem.at[1])
    for copy in (plan_in, lens_in, k_own, v_own, q_in, g_in):
        copy.start()

    pl.semaphore_wait(barrier, n_cp - 1 + jnp.where(sec > 0, n_cp, 0))

    def kv_copies(d, source):
        rows = pl.ds(pl.multiple_of(source * tokens, tokens), tokens)
        return [
            pltpu.make_async_remote_copy(
                src_ref=hbm.at[0], dst_ref=full.at[rows],
                send_sem=kv_send.at[i, d], recv_sem=kv_recv.at[i, source],
                device_id={"cp": d}, device_id_type=MESH,
            )
            for i, (hbm, full) in enumerate(((k_hbm, kall), (v_hbm, vall)))
        ]

    for d in reversed(range(1, n_cp)):
        @pl.when(me < d)
        def _():
            for copy in kv_copies(d, me):
                copy.start()

    odd = me % 2

    @pl.when(sec == n_pp - 1)
    def _():
        land[...] = jnp.zeros_like(land)

    plan_in.wait()
    lens_in.wait()

    def taken_of(slot):
        taken = jnp.zeros_like(slot)
        for d in range(n_cp):
            inverse = jnp.int32(0)
            for j in range(1, n_cp):
                inverse = inverse + jnp.where(plan_ref[me, j] == d, j, 0)
            taken = jnp.where(slot == d, inverse, taken)
        return taken

    row = lax.broadcasted_iota(jnp.int32, (tokens, tokens), 0)
    col = lax.broadcasted_iota(jnp.int32, (tokens, tokens), 1)
    row_slot = row // block_rows
    local = taken_of(row_slot) * block_rows + (row - row_slot * block_rows)
    perm = jnp.where(local == col, 1.0, 0.0).astype(BF16)

    lane = lax.broadcasted_iota(jnp.int32, (1, tokens), 1)
    lane_slot = lane // block_rows
    q_pos = me * tokens + taken_of(lane_slot) * block_rows + (lane - lane_slot * block_rows)
    begin = jnp.zeros_like(q_pos)
    end = jnp.int32(0)
    for i in range(ndoc):
        end = end + lens_ref[i]
        begin = jnp.where(q_pos >= end, end, begin)
    for s in range(n_cp):
        k_pos = lax.broadcasted_iota(jnp.int32, (tokens, tokens), 0) + s * tokens
        seen = (k_pos >= begin) & (k_pos <= q_pos)
        bias[s * tokens:(s + 1) * tokens, :] = jnp.where(seen, 0.0, -jnp.inf)

    q_in.wait()
    g_in.wait()

    def stack(raw, out, c):
        width = 4 * hd
        cols = pl.ds(pl.multiple_of(c * width, width), width)
        moved = jnp.dot(perm, raw[:, cols], preferred_element_type=F32).astype(BF16)
        for h in range(4):
            at = pl.ds(pl.multiple_of((c * 4 + h) * tokens, tokens), tokens)
            out[at, :] = moved[:, h * hd:(h + 1) * hd]

    def stack_both(c, carry):
        stack(qraw, qs, c)
        stack(graw, gs, c)
        return carry

    lax.fori_loop(0, heads // 4, stack_both, 0)
    k_own.wait()
    v_own.wait()

    pieces = heads // chunk
    relayed = pieces // 2
    crosses = (sec > 0) & (sec % 2 == 0)
    forwards = (sec % 2 == 1) & (sec < n_pp - 1)
    before = lax.rem(sec + n_pp - 1, n_pp)
    my_block = pl.ds(pl.multiple_of(me * block_rows, block_rows), block_rows)

    def dq_copy(d, piece):
        return pltpu.make_async_remote_copy(
            src_ref=stag.at[piece, pl.ds(pl.multiple_of(d * block_rows, block_rows), block_rows)],
            dst_ref=land.at[piece, my_block],
            send_sem=dq_send, recv_sem=dq_recv.at[piece],
            device_id={"pp": before, "cp": d}, device_id_type=MESH,
        )

    def cross_copy(off, piece):
        d = lax.rem(me + off, n_cp)
        return pltpu.make_async_remote_copy(
            src_ref=stag.at[piece, pl.ds(pl.multiple_of(d * block_rows, block_rows), block_rows)],
            dst_ref=relay.at[piece, pl.ds((off - 1) * block_rows, block_rows)],
            send_sem=dq_send, recv_sem=relay_recv.at[piece],
            device_id={"pp": before}, device_id_type=MESH,
        )

    def forward(piece):
        pltpu.make_async_remote_copy(
            src_ref=relay.at[piece], dst_ref=relay.at[piece], send_sem=dq_send, recv_sem=relay_recv.at[piece],
            device_id={"pp": before}, device_id_type=MESH,
        ).wait_recv()
        for off in range(1, n_cp):
            pltpu.make_async_remote_copy(
                src_ref=relay.at[piece, pl.ds((off - 1) * block_rows, block_rows)],
                dst_ref=land.at[piece, my_block],
                send_sem=relay_send, recv_sem=dq_recv.at[piece],
                device_id={"cp": lax.rem(me + off, n_cp)}, device_id_type=MESH,
            ).start()

    def send_dq(piece):
        @pl.when(crosses & (piece < relayed))
        def _():
            for off in range(1, n_cp):
                cross_copy(off, piece).start()
            dq_copy(me, piece).start()

        @pl.when((sec > 0) & jnp.logical_not(crosses & (piece < relayed)))
        def _():
            for d in range(n_cp):
                dq_copy(d, piece).start()

        @pl.when(forwards & (piece >= 2) & (piece < relayed + 2))
        def _():
            forward(piece - 2)

    def d_copy(kb):
        slot = odd * kb + (1 - odd) * me
        target = odd * (me - 1) + (1 - odd) * kb
        return pltpu.make_async_remote_copy(
            src_ref=dsend.at[pl.ds(kb * tokens, tokens)],
            dst_ref=drecv.at[pl.ds(pl.multiple_of(slot * tokens, tokens), tokens)],
            send_sem=d_send.at[kb], recv_sem=d_recv.at[slot],
            device_id={"cp": target}, device_id_type=MESH,
        )

    def d_arrived(slot):
        at = pl.ds(slot * tokens, tokens)
        pltpu.make_async_remote_copy(
            src_ref=dsend.at[at], dst_ref=drecv.at[at], send_sem=d_send.at[slot], recv_sem=d_recv.at[slot],
            device_id={"cp": lax.rem(me + 1, n_cp)}, device_id_type=MESH,
        ).wait_recv()
        return drecv[slot * tokens:(slot + 1) * tokens, :].astype(F32)

    for s in range(n_cp - 1):
        @pl.when(s < me)
        def _():
            for copy in kv_copies(n_cp - 1, s):
                copy.wait_recv()

    def work(group):
        shards = (group + 1) * per_group
        count = shards * tokens
        for s in range(group * per_group + 1, shards):
            @pl.when(me < s)
            def _():
                kall[s * tokens:(s + 1) * tokens, :] = jnp.zeros((tokens, kall.shape[1]), BF16)
                vall[s * tokens:(s + 1) * tokens, :] = jnp.zeros((tokens, vall.shape[1]), BF16)

        def one_kv(kv, carry):
            kv_cols = pl.ds(pl.multiple_of(kv * hd, hd), hd)
            for s in range(shards):
                at = slice(s * tokens, (s + 1) * tokens)
                kt[:, at] = kall[at, kv_cols].astype(F32).T.astype(BF16)

            def one_chunk(c, carry):
                for pair in range(chunk // 2):
                    first = c * chunk + pair * 2
                    rows = pl.ds(pl.multiple_of((kv * group_heads + first) * tokens, 2 * tokens), 2 * tokens)
                    kept = pl.ds(pl.multiple_of(first * tokens, 2 * tokens), 2 * tokens)
                    seen = bias[0:count, :]
                    score = lax.dot_general(kall[0:count, kv_cols], qs[rows, :], NT, preferred_element_type=F32)
                    score = score + jnp.concatenate([seen, seen], axis=1)
                    dprob = lax.dot_general(vall[0:count, kv_cols], gs[rows, :], NT, preferred_element_type=F32)
                    top = jnp.max(score, axis=0, keepdims=True)
                    expo = jnp.exp2((score - top) * (scale * math.log2(math.e)))
                    inverse = 1.0 / jnp.sum(expo, axis=0, keepdims=True)
                    delta = jnp.sum(expo * dprob, axis=0, keepdims=True) * inverse
                    pst[0:count, kept] = (expo * inverse).astype(BF16)
                    dscore = (expo * (inverse * scale) * (dprob - delta)).astype(BF16)
                    dst[0:count, kept] = dscore

                    @pl.when(sec > 0)
                    def _():
                        dqt = jnp.dot(kt[:, 0:count], dscore, preferred_element_type=F32)
                        for h in range(2):
                            at = slice((pair * 2 + h) * hd, (pair * 2 + h + 1) * hd)
                            stag[kv * (group_heads // chunk) + c, :, at] = dqt[:, h * tokens:(h + 1) * tokens].T.astype(stag.dtype)

                send_dq(kv * (group_heads // chunk) + c)
                return carry

            lax.fori_loop(0, group_heads // chunk, one_chunk, 0)

            all_rows = pl.ds(pl.multiple_of(kv * group_heads * tokens, group_heads * tokens), group_heads * tokens)
            term_cols = pl.ds(pl.multiple_of(kv * 2 * hd, 2 * hd), 2 * hd)
            for kb in range(shards):
                at = slice(kb * tokens, (kb + 1) * tokens)
                dkey = jnp.dot(dst[at, :], qs[all_rows, :], preferred_element_type=F32)
                dvalue = jnp.dot(pst[at, :], gs[all_rows, :], preferred_element_type=F32)
                both = jnp.concatenate([dkey, dvalue], axis=1)

                @pl.when(me == kb)
                def _():
                    acc[:, term_cols] = both

                @pl.when(kb < me)
                def _():
                    dsend[at, term_cols] = both.astype(BF16)

                if nkv == 1:
                    @pl.when((kb < me) & (odd == 1))
                    def _():
                        d_copy(kb).start()

            return carry

        if nkv == 1:
            one_kv(0, 0)
        else:
            lax.fori_loop(0, nkv, one_kv, 0)

    for group in range(groups):
        pl.when(my_group == group)(functools.partial(work, group))

    for kb in range(n_cp - 1):
        at = slice(kb * tokens, (kb + 1) * tokens)

        @pl.when((kb < me) & (odd == 0))
        def _():
            dsend[at, :] = (dsend[at, :].astype(F32) + d_arrived(kb)).astype(BF16)
            d_copy(kb).start()

        if nkv > 1:
            @pl.when((kb < me) & (odd == 1))
            def _():
                d_copy(kb).start()

    for e in range(0, n_cp, 2):
        @pl.when(me <= e)
        def _():
            acc[...] += d_arrived(e)

    for kv in range(nkv):
        kg_ref[0, :, kv * hd:(kv + 1) * hd] = acc[:, kv * 2 * hd:kv * 2 * hd + hd].astype(BF16)
        vg_ref[0, :, kv * hd:(kv + 1) * hd] = acc[:, kv * 2 * hd + hd:(kv + 1) * 2 * hd].astype(BF16)

    for d in range(n_cp):
        @pl.when(me < d)
        def _():
            for copy in kv_copies(d, me):
                copy.wait_send()

        @pl.when(d < me)
        def _():
            d_copy(d).wait_send()

    @pl.when(forwards)
    def _():
        pltpu.make_async_remote_copy(
            src_ref=relay, dst_ref=relay, send_sem=relay_send, recv_sem=relay_recv.at[0],
            device_id={"pp": before}, device_id_type=MESH,
        ).wait_send()

    @pl.when(sec > 0)
    def _():
        pltpu.make_async_remote_copy(
            src_ref=stag, dst_ref=land, send_sem=dq_send, recv_sem=dq_recv.at[0],
            device_id={"pp": lax.rem(sec + n_pp - 1, n_pp)}, device_id_type=MESH,
        ).wait_send()

    outs = []
    for piece in range(pieces):
        @pl.when(sec < n_pp - 1)
        def _():
            pltpu.make_async_remote_copy(
                src_ref=stag.at[piece], dst_ref=land.at[piece], send_sem=dq_send, recv_sem=dq_recv.at[piece],
                device_id={"pp": lax.rem(sec + n_pp - 1, n_pp)}, device_id_type=MESH,
            ).wait_recv()

        cols = pl.ds(piece * chunk * hd, chunk * hd)
        outs.append(pltpu.make_async_copy(land.at[piece], handed.at[0, :, cols], out_sem.at[piece]))
        outs[-1].start()
    for copy in outs:
        copy.wait()


def finish(handed, kg, vg, handed_out, kg_out, vg_out, handed_buf, kg_buf, vg_buf, sem):
    rows = handed.shape[1] // 4
    trips = [(kg, kg_buf, kg_out), (vg, vg_buf, vg_out)]
    for i in range(4):
        at = (slice(None), pl.ds(i * rows, rows))
        trips.append((handed.at[at], handed_buf.at[at], handed_out.at[at]))
    loads = [pltpu.make_async_copy(a, b, sem.at[0, i]) for i, (a, b, _) in enumerate(trips)]
    stores = [pltpu.make_async_copy(b, c, sem.at[1, i]) for i, (_, b, c) in enumerate(trips)]
    for load in loads:
        load.start()
    for load, store in zip(loads, stores):
        load.wait()
        store.start()
    for store in stores:
        store.wait()


def body(n_pp, n_cp, n_tp, query, key, value, out_grad, lengths, plan):
    tokens, width = query.shape[1], query.shape[2]
    kv_width = key.shape[2]
    hd = 128
    heads, nkv = width // hd, kv_width // hd
    groups = min(n_cp, 4)
    block_rows = tokens // n_cp
    seq = n_cp * tokens
    wide = BF16 if block_rows % 16 == 0 else F32
    chunk = 4
    group_rows = heads // nkv * tokens
    sizes = (n_pp, n_cp, tokens, heads, nkv, hd, lengths.shape[0], groups, chunk)
    hbm = pl.BlockSpec(memory_space=pltpu.HBM)
    vmem = pl.BlockSpec(memory_space=pltpu.VMEM)
    dma = pltpu.SemaphoreType.DMA
    handed, key_grad, value_grad = pl.pallas_call(
        functools.partial(kernel, sizes),
        out_shape=(
            jax.ShapeDtypeStruct(query.shape, wide),
            jax.ShapeDtypeStruct(key.shape, BF16),
            jax.ShapeDtypeStruct(value.shape, BF16),
        ),
        in_specs=[hbm] * 6,
        out_specs=(hbm, vmem, vmem),
        scratch_shapes=[
            pltpu.SMEM(plan.shape, jnp.int32),
            pltpu.SMEM(lengths.shape, jnp.int32),
            pltpu.VMEM((tokens, width), BF16),
            pltpu.VMEM((tokens, width), BF16),
            pltpu.VMEM((heads * tokens, hd), BF16),
            pltpu.VMEM((heads * tokens, hd), BF16),
            pltpu.VMEM((seq, kv_width), BF16),
            pltpu.VMEM((seq, kv_width), BF16),
            pltpu.VMEM((hd, seq), BF16),
            pltpu.VMEM((seq, tokens), F32),
            pltpu.VMEM((seq, group_rows), BF16),
            pltpu.VMEM((seq, group_rows), BF16),
            pltpu.VMEM((heads // chunk, tokens, chunk * hd), wide),
            pltpu.VMEM((heads // chunk, tokens, chunk * hd), wide),
            pltpu.VMEM((heads // chunk // 2, tokens - block_rows, chunk * hd), wide),
            pltpu.VMEM((tokens, 2 * kv_width), F32),
            pltpu.VMEM((seq, 2 * kv_width), BF16),
            pltpu.VMEM((seq, 2 * kv_width), BF16),
            dma((2,)), dma((2,)), dma((2, n_cp)), dma((2, n_cp)),
            dma, dma((heads // chunk,)), dma, dma((heads // chunk // 2,)), dma((n_cp,)), dma((n_cp,)), dma((heads // chunk,)), dma((2,)),
        ],
        compiler_params=pltpu.CompilerParams(
            collective_id=0, has_side_effects=True, vmem_limit_bytes=VMEM
        ),
        cost_estimate=pl.CostEstimate(
            flops=10 * tokens * heads * seq * hd, bytes_accessed=6 * tokens * width,
            transcendentals=tokens * heads * seq,
        ),
    )(plan, lengths, query, key, value, out_grad)
    if wide != BF16:
        return handed.astype(BF16), key_grad, value_grad
    results = (handed, key_grad, value_grad)
    return pl.pallas_call(
        finish,
        out_shape=tuple(jax.ShapeDtypeStruct(r.shape, r.dtype) for r in results),
        in_specs=[hbm] * 3,
        out_specs=(hbm,) * 3,
        scratch_shapes=[pltpu.VMEM(r.shape, r.dtype) for r in results] + [dma((2, 6))],
        compiler_params=pltpu.CompilerParams(vmem_limit_bytes=VMEM),
    )(*results)


def solution(mesh):
    spec = P("pp", "cp", "tp")
    sizes = (mesh.shape["pp"], mesh.shape["cp"], mesh.shape["tp"])
    return jax.shard_map(
        functools.partial(body, *sizes),
        mesh=mesh,
        in_specs=(spec, spec, spec, spec, P(), P()),
        out_specs=(spec, spec, spec),
        check_vma=False,
    )
```
